128 devices in a mesh: comp: 2 (over z_hi), dom: 64 (over x, y, z_lo, core).
Axes of the slice: x: 4, y: 4, z: 4 (z_hi: 2, z_lo: 2; z = z_hi * 2 + z_lo), core: 2. Of those that a mesh axis runs over, the one named last changes fastest.
Arguments:
- prognostic: float32 [2, 144, 65536], P('comp', None, 'dom'), may hold values from -6 to 6
- neighbours: int32 [2, 6, 65536], P('comp', None, 'dom'), may hold values from 0 to 1535, as said below
- diffusivity: float32 [2, 6, 65536], P('comp', None, 'dom'), may hold values from 0.02 to 0.15
- vertical: float32 [2, 144, 144], P('comp'), may hold values from -0.09375 to 0.09375
- export_map: float32 [2, 48, 144], P('comp'), may hold values from -0.5 to 0.5
- import_map: float32 [2, 144, 48], P('comp'), may hold values from -0.875 to 0.875
- ocean_mask: int32 [2, 65536], P('comp', 'dom'), may hold values 0 or 1
- source_blocks: int32 [2, 64, 3], P('comp', 'dom'), may hold values from 0 to 63, as said below
- remap_index: int32 [2, 16, 65536], P('comp', None, 'dom'), may hold values from 0 to 3071
- remap_weights: float32 [2, 16, 65536], P('comp', None, 'dom'), may hold values from -1.5 to 1.5
Outputs:
- stepped: float32 [2, 144, 65536], P('comp', None, 'dom')
- imported: float32 [2, 48, 65536], P('comp', None, 'dom')
The draws below stay inside these ranges and needn't reach their ends.
Inputs may be any that keep to these rules, and one draw needn't show every extreme that they name: `neighbours`: an index e names cell e - 256 of the block, counting into the 256 last cells of the block before and the 256 first cells of the block after (the blocks wrap around); it never names the cell itself, and the cell named lies at most 256 positions from the cell itself. `source_blocks`: the entries for block j are 3 distinct blocks within 3 of j counted cyclically, j itself among them.
All inputs are finite; a program needn't handle non-finite values. No bound on the sum of `ocean_mask` on one device may be relied on, other than what follows from the above.
Results may differ from the reference program's by a relative error of at most 0.0001.
Values sent between devices are 32-bit elements; how exact they have to be, the bound alone decides.
A program may use at most 128 MiB of HBM per device.

```python
import math
import jax
import jax.numpy as jnp
from jax import lax

CELLS = 1024
NBR = 6
FLUX = 48
TAPS = 16
REACH = 3
SOURCES = 3
STEPS_OCN = 3
NV = 144
HALO = 256
CELLS_TOT = 65536
N_DOM = 64


def draw_neighbours(key, part):
    key = jax.random.fold_in(key, 11)
    first_key, second_key = jax.random.split(key)
    shape = (2, NBR, CELLS_TOT)
    distance = jax.random.randint(first_key, shape, 1, HALO + 1)
    direction = jax.random.randint(second_key, shape, 0, 2) * 2 - 1
    local = jnp.arange(CELLS_TOT, dtype=jnp.int32) % CELLS
    values = local[None, None, :] + HALO + direction * distance
    slot_zero = (jnp.arange(NBR, dtype=jnp.int32) == 0)[None, :, None]
    values = jnp.where(slot_zero & (local == 0)[None, None, :], 0, values)
    values = jnp.where(slot_zero & (local == CELLS - 1)[None, None, :], CELLS + 2 * HALO - 1, values)
    return values.astype(jnp.int32)


def draw_source_blocks(key, part):
    key = jax.random.fold_in(key, 23)
    first_key, second_key = jax.random.split(key)
    width = 2 * REACH
    scores = jax.random.randint(first_key, (2, N_DOM, width), 0, 2 ** 20) * width + jnp.arange(width, dtype=jnp.int32)
    chosen = jnp.argsort(scores, axis=-1)[..., :SOURCES - 1].astype(jnp.int32)
    offsets = jnp.where(chosen < REACH, chosen - REACH, chosen - REACH + 1)
    offsets = jnp.concatenate([jnp.zeros((2, N_DOM, 1), jnp.int32), offsets], axis=-1)
    slot_scores = jax.random.randint(second_key, (2, N_DOM, SOURCES), 0, 2 ** 20) * SOURCES + jnp.arange(SOURCES, dtype=jnp.int32)
    order = jnp.argsort(slot_scores, axis=-1).astype(jnp.int32)
    offsets = jnp.take_along_axis(offsets, order, axis=-1)
    blocks = jnp.arange(N_DOM, dtype=jnp.int32)[None, :, None]
    return ((blocks + offsets) % N_DOM).astype(jnp.int32)


def with_ends(entries, key, least, high):
    index_at = [jax.random.randint(jax.random.fold_in(key, axis), (), 0, length) for axis, length in enumerate(entries.shape)]
    longest = entries.shape.index(max(entries.shape))
    next_to = index_at[:longest] + [(index_at[longest] + 1) % entries.shape[longest]] + index_at[longest + 1:]
    return entries.at[tuple(index_at)].set(least).at[tuple(next_to)].set(high)


def levels(stream_key, shape, pieces, smallest, high):
    def one(position, shards_of):
        draws = jax.random.uniform(jax.random.fold_in(jax.random.fold_in(stream_key, 6), position), (shards_of,), jnp.float32, smallest / len(pieces), high / len(pieces))
        return jnp.repeat(jnp.exp(draws), shape[position] // shards_of).reshape((-1,) + (1,) * (len(shape) - position - 1))

    level = one(*pieces[0])
    for cut in pieces[1:]:
        level = level * one(*cut)
    return level


def bell_draw(rng, dims, spread, bound, cuts=(), kind=jnp.bfloat16):
    level = levels(rng, dims, cuts, -0.22, 0.18) if cuts else 1.0
    values = jax.random.normal(rng, dims, jnp.float32) * spread * level
    return jnp.minimum(jnp.maximum(values, -bound), bound).astype(kind)


def setup_inputs(seed: int = 0) -> dict:
    key_of = jax.random.split(jax.random.key(seed), 11)
    return {
        "prognostic": bell_draw(key_of[0], (2, NV, CELLS_TOT), 1.0, 6.0, ((0, 2), (2, 64)), jnp.float32),
        "neighbours": draw_neighbours(jax.random.fold_in(key_of[10], 71), 0),
        "diffusivity": jnp.clip(jnp.exp(math.log(0.15) - 2.014903 * jax.random.uniform(key_of[2], (2, NBR, CELLS_TOT), jnp.float32) ** levels(key_of[2], (2, NBR, CELLS_TOT), ((0, 2), (2, 64)), -0.2, 0.2)), 0.02, 0.15),
        "vertical": bell_draw(key_of[3], (2, NV, NV), (25 * NV) ** -0.5, 0.09375, ((0, 2),), jnp.float32),
        "export_map": bell_draw(key_of[4], (2, FLUX, NV), NV ** -0.5, 0.5, ((0, 2),), jnp.float32),
        "import_map": bell_draw(key_of[5], (2, NV, FLUX), FLUX ** -0.5, 0.875, ((0, 2),), jnp.float32),
        "ocean_mask": with_ends((jax.random.randint(key_of[6], (2, CELLS_TOT), 0, 4) < 3).astype(jnp.int32), jax.random.fold_in(key_of[6], 1), 0, 1),
        "source_blocks": draw_source_blocks(jax.random.fold_in(key_of[10], 71), 0),
        "remap_index": with_ends(jax.random.randint(key_of[8], (2, TAPS, CELLS_TOT), 0, SOURCES * CELLS), jax.random.fold_in(key_of[8], 1), 0, (SOURCES * CELLS) - 1).astype(jnp.int32),
        "remap_weights": bell_draw(key_of[9], (2, TAPS, CELLS_TOT), TAPS ** -0.5, 1.5, ((0, 2), (2, 64)), jnp.float32),
    }


def remap_into(source, owners, index, weights):
    blocks = source.reshape(FLUX, N_DOM, CELLS).transpose(1, 0, 2)
    index_blocks = index.reshape(TAPS, N_DOM, CELLS).transpose(1, 0, 2)
    weight_blocks = weights.reshape(TAPS, N_DOM, CELLS).transpose(1, 0, 2)

    def one_block(block):
        picked = blocks[owners[block]]
        flat = picked.transpose(1, 0, 2).reshape(FLUX, SOURCES * CELLS)
        taken = jnp.take(flat, index_blocks[block], axis=1)
        return jnp.sum(weight_blocks[block][None] * taken, axis=1)

    result = lax.map(one_block, jnp.arange(N_DOM, dtype=jnp.int32))
    return result.transpose(1, 0, 2).reshape(FLUX, CELLS_TOT)


def reference(prognostic, neighbours, diffusivity, vertical, export_map, import_map, ocean_mask, source_blocks, remap_index, remap_weights):
    exported = [ocean_mask[which].astype(jnp.float32) * jnp.dot(export_map[which], prognostic[which], precision=lax.Precision.HIGHEST) for which in range(2)]
    imported = [remap_into(exported[1 - which], source_blocks[which], remap_index[which], remap_weights[which]) for which in range(2)]
    starts = (jnp.arange(CELLS_TOT, dtype=jnp.int32) // CELLS) * CELLS
    stepped = []
    for which in range(2):
        forcing = jnp.dot(import_map[which], imported[which], precision=lax.Precision.HIGHEST)
        global_index = (starts[None, :] + neighbours[which] - HALO) % CELLS_TOT
        current = prognostic[which]
        for substep in range(1 if which == 0 else STEPS_OCN):
            gathered = current[:, global_index]
            diffusion = jnp.sum(diffusivity[which][None] * (gathered - current[:, None, :]), axis=1)
            current = current + diffusion + jnp.dot(vertical[which], current, precision=lax.Precision.HIGHEST) + forcing
        stepped.append(current)
    return jnp.stack(stepped), jnp.stack(imported)
```

```python
import jax
import jax.numpy as jnp
from jax import lax
from jax.experimental import pallas as pl
from jax.experimental.pallas import tpu as pltpu
from jax.sharding import PartitionSpec as P

CELLS = 1024
NBR = 6
FLUX = 48
TAPS = 16
SOURCES = 3
NV = 144
HALO = 256
N_DOM = 64
TILE = 128
ROWS = 256
GROUP = 256
WINDOW = GROUP + 2 * HALO
MESH = pl.DeviceIdType.MESH
f32 = jnp.float32
bf16 = jnp.bfloat16


def split(x):
    high = x.astype(bf16)
    return high, (x - high.astype(f32)).astype(bf16)


def dot(a, b):
    return jnp.dot(a, b, preferred_element_type=f32)


def dot3(a, b):
    ah, al = split(a)
    bh, bl = split(b)
    return dot(ah, bh) + dot(al, bh) + dot(ah, bl)


def row_iota(n):
    return lax.broadcasted_iota(jnp.int32, (16, TILE), 0).astype(f32)


def spread(places, highs, lows, rows):
    base = row_iota(rows)
    count = rows // 16
    keys = [(base + 16.0 * r).astype(bf16) for r in range(count)]
    high = [jnp.zeros((16, TILE), bf16)] * count
    low = [jnp.zeros((16, TILE), bf16)] * count
    for place, h, l in zip(places, highs, lows):
        for r in range(count):
            hit = place == keys[r]
            high[r] = jnp.where(hit, h, high[r])
            low[r] = jnp.where(hit, l, low[r])
    return high, low


def kernel(
    prog, nbr, diff, vert, emap, imap, mask, blocks, ridx, rw,
    out, imported,
    exported, slots, ph, pl_, place, wh, wl,
    table, nh, nl, halo_l, halo_r, ub, states, vst, dst,
    xs, ie, ine, far_l, far_r,
    slot_send, slot_recv, uh_send, uh_recv, tab_send, tab_recv, i_send, i_recv,
):
    c = lax.axis_index("comp")
    d = lax.axis_index("dom")
    k = lax.rem(d, 2)
    m = d // 2
    zl = lax.rem(m, 2)
    left = (c, lax.rem(d + N_DOM - 1, N_DOM))
    right = (c, lax.rem(d + 1, N_DOM))
    sibling = (c, d + 1 - 2 * k)
    across = (1 - c, d)
    beside = (1 - c, 2 * (m + 1 - 2 * zl) + k)
    up = lax.rem(d + 4, N_DOM)
    down = lax.rem(d + N_DOM - 4, N_DOM)

    barrier = pltpu.get_barrier_semaphore()
    for peer in (left, right, across, beside, (c, up), (c, down)):
        pl.semaphore_signal(barrier, inc=1, device_id=peer, device_id_type=MESH)

    emap_h, emap_l = split(emap[...])
    est = jnp.concatenate([emap_h, emap_l], axis=0)
    for g in range(4):
        cols = pl.ds(g * GROUP, GROUP)
        uh, ul = split(prog[:, cols])
        ub[0:NV, pl.ds((g + 1) * GROUP, GROUP)] = uh
        ub[NV : 2 * NV, pl.ds((g + 1) * GROUP, GROUP)] = ul
        both = dot(est, uh)
        exported[:, cols] = mask[:, cols].astype(f32) * (
            both[0:FLUX] + both[FLUX : 2 * FLUX] + dot(emap_h, ul)
        )

    def send(src, dst, s_sem, r_sem, peer):
        copy = pltpu.make_async_remote_copy(
            src_ref=src, dst_ref=dst, send_sem=s_sem, recv_sem=r_sem,
            device_id=peer, device_id_type=MESH,
        )
        copy.start()
        return copy

    def to_slot(src, slot, number, peer):
        return send(src, slots.at[slot], slot_send.at[number], slot_recv.at[slot], peer)

    def arrived(slot):
        pltpu.make_async_remote_copy(
            src_ref=slots.at[slot], dst_ref=slots.at[slot], send_sem=slot_send.at[0],
            recv_sem=slot_recv.at[slot], device_id=sibling, device_id_type=MESH,
        ).wait_recv()

    own = 3 + k
    from_z = 5 + k - 4 * zl
    from_y = 1 + k + 4 * zl
    edge = 7 - 7 * k

    pl.semaphore_wait(barrier, 6)
    slot_copies = [
        to_slot(exported, own, 0, across),
        to_slot(exported, from_y, 1, beside),
    ]

    def send_halo(source, level):
        return [
            send(source.at[:, pl.ds(0, HALO)], halo_r.at[level], uh_send.at[2 * level],
                 uh_recv.at[2 * level], left),
            send(source.at[:, pl.ds(CELLS - HALO, HALO)], halo_l.at[level], uh_send.at[2 * level + 1],
                 uh_recv.at[2 * level + 1], right),
        ]

    halo0 = send_halo(prog, 0)

    places = []
    weights = []
    total = jnp.zeros((1, CELLS), f32)
    for s in range(NBR):
        e = nbr[s : s + 1, :]
        w = diff[s : s + 1, :]
        total = total + w
        double = jnp.zeros((1, CELLS), jnp.bool_)
        for t in range(s):
            same = places[t] == e
            weights[t] = weights[t] + jnp.where(same, w, 0.0)
            double = jnp.logical_or(double, same)
        places.append(jnp.where(double, -4096, e))
        weights.append(w)
    for g in range(4):
        cols = slice(g * GROUP, (g + 1) * GROUP)
        for s in range(NBR):
            table[g + 1, s : s + 1, :] = (places[s][:, cols] - g * GROUP).astype(f32)
            table[g + 1, 8 + s : 9 + s, :] = weights[s][:, cols]
        table[g + 1, 6:7, :] = (lax.broadcasted_iota(jnp.int32, (1, GROUP), 1) + HALO).astype(f32)
        table[g + 1, 14:15, :] = 1.0 - total[:, cols]
    tab_copies = [
        send(table.at[4], table.at[0], tab_send.at[0], tab_recv.at[0], right),
        send(table.at[1], table.at[5], tab_send.at[1], tab_recv.at[1], left),
    ]

    idx = ridx[...]
    w = rw[...]
    tap = lax.broadcasted_iota(jnp.int32, (TAPS, CELLS), 0)
    total_w = w
    double = tap < 0
    for s in range(1, TAPS):
        same = idx == pltpu.roll(idx, s, 0)
        total_w = total_w + jnp.where(same, pltpu.roll(w, s, 0), 0.0)
        double = jnp.logical_or(double, jnp.logical_and(same, tap >= s))
    place[...] = jnp.where(double, -4096, idx).astype(f32)
    for t in range(TAPS):
        h, l = split(jnp.broadcast_to(total_w[t : t + 1, :], (16, CELLS)))
        wh[16 * t : 16 * t + 16, :] = h
        wl[16 * t : 16 * t + 16, :] = l

    def build_remap(first, last):
        def chunk(i, carry):
            row = (i // 8) * ROWS
            cols = pl.ds(pl.multiple_of(lax.rem(i, 8) * TILE, TILE), TILE)
            base = row.astype(f32)
            at = [
                (jnp.broadcast_to(place[t : t + 1, cols], (16, TILE)) - base).astype(bf16)
                for t in range(TAPS)
            ]
            high, low = spread(
                at,
                [wh[16 * t : 16 * t + 16, cols] for t in range(TAPS)],
                [wl[16 * t : 16 * t + 16, cols] for t in range(TAPS)],
                ROWS,
            )
            for r in range(ROWS // 16):
                rows = pl.ds(pl.multiple_of(row + 16 * r, 16), 16)
                ph[rows, cols] = high[r]
                pl_[rows, cols] = low[r]
            return carry

        lax.fori_loop(first, last, chunk, 0)

    def build_neighbour(first, last):
        def chunk(i, carry):
            g = i // 6
            half = lax.rem(i, 6) // 3
            row = lax.rem(i, 3) * ROWS
            cols = pl.ds(pl.multiple_of(half * TILE, TILE), TILE)
            base = row.astype(f32)
            at, highs, lows = [], [], []
            for s in range(NBR + 1):
                at.append((jnp.broadcast_to(table[g, s : s + 1, cols], (16, TILE)) - base).astype(bf16))
                h, l = split(jnp.broadcast_to(table[g, 8 + s : 9 + s, cols], (16, TILE)))
                highs.append(h)
                lows.append(l)
            high, low = spread(at, highs, lows, ROWS)
            for r in range(ROWS // 16):
                rows = pl.ds(pl.multiple_of(row + 16 * r, 16), 16)
                nh[g, rows, cols] = high[r]
                nl[g, rows, cols] = low[r]
            return carry

        lax.fori_loop(6 * first, 6 * last, chunk, 0)

    vh, vl = split(vert[...])
    vst[0:NV, :] = vh
    vst[NV : 2 * NV, :] = vl

    def advance(level):
        for side, start in ((halo_l, 0), (halo_r, 5 * GROUP)):
            h, l = split(side[level])
            ub[0:NV, pl.ds(start, GROUP)] = h
            ub[NV : 2 * NV, pl.ds(start, GROUP)] = l

        def group(g, carry):
            window = pl.ds(pl.multiple_of(g * GROUP, GROUP), WINDOW)
            mid = pl.ds(pl.multiple_of((g + 1) * GROUP, GROUP), GROUP)
            a = dot(ub[:, window], nh[g + 1])
            b = dot(vst[...], ub[0:NV, mid])
            total = a[0:NV] + a[NV : 2 * NV] + dot(ub[0:NV, window], nl[g + 1])
            total = total + (b[0:NV] + b[NV : 2 * NV] + dot(vst[0:NV, :], ub[NV : 2 * NV, mid]))
            states[level, :, pl.ds(pl.multiple_of(g * GROUP, GROUP), GROUP)] = total
            return carry

        lax.fori_loop(0, 4, group, 0)

    def refill(level):
        def group(g, carry):
            mid = pl.ds(pl.multiple_of((g + 1) * GROUP, GROUP), GROUP)
            h, l = split(states[level, :, pl.ds(pl.multiple_of(g * GROUP, GROUP), GROUP)])
            ub[0:NV, mid] = h
            ub[NV : 2 * NV, mid] = l
            return carry

        lax.fori_loop(0, 4, group, 0)

    def wait_recv(copies):
        for copy in copies:
            copy.wait_recv()

    def wait_send(copies):
        for copy in copies:
            copy.wait_send()

    build_neighbour(1, 5)
    wait_recv(halo0)
    advance(0)

    @pl.when(c == 1)
    def _():
        first = send_halo(states.at[0], 1)
        wait_send(first)

    arrived(own)
    arrived(from_z)
    along = lax.select(zl == 0, up, down)
    slot_copies.append(to_slot(slots.at[from_z], from_y, 2, (c, along)))
    slot_copies.append(to_slot(slots.at[own], edge, 3, (c, lax.select(k == 1, up, down))))
    slot_copies.append(to_slot(slots.at[own], own, 4, sibling))
    slot_copies.append(to_slot(slots.at[from_z], from_z, 5, sibling))

    build_remap(0, 32)

    @pl.when(c == 1)
    def _():
        refill(0)
        for side in range(2):
            pltpu.make_async_remote_copy(
                src_ref=halo_l.at[1], dst_ref=(halo_r, halo_l)[side].at[1], send_sem=uh_send.at[2 + side],
                recv_sem=uh_recv.at[2 + side], device_id=left, device_id_type=MESH,
            ).wait_recv()
        advance(1)
        second = send_halo(states.at[1], 2)
        wait_send(second)

    arrived(from_y)
    arrived(edge)
    slot_copies.append(to_slot(slots.at[from_y], from_y, 6, sibling))
    slot_copies.append(to_slot(slots.at[edge], edge, 7, sibling))

    build_remap(32, 96)

    m0 = imap[...]

    @pl.when(c == 0)
    def _():
        h, l = split(m0)
        dst[0, 0:NV, :] = h
        dst[0, NV : 2 * NV, :] = l

    @pl.when(c == 1)
    def _():
        refill(1)
        for side in range(2):
            pltpu.make_async_remote_copy(
                src_ref=halo_l.at[2], dst_ref=(halo_r, halo_l)[side].at[2], send_sem=uh_send.at[4 + side],
                recv_sem=uh_recv.at[4 + side], device_id=left, device_id_type=MESH,
            ).wait_recv()
        advance(2)
        v = vert[...]
        vm = dot3(v, m0)
        vvm = dot3(v, vm)
        for number, value in enumerate((m0 + vm + vvm, m0 + 2.0 * vm, m0)):
            h, l = split(value)
            dst[number, 0:NV, :] = h
            dst[number, NV : 2 * NV, :] = l
        wait_recv(tab_copies)
        build_neighbour(0, 1)
        build_neighbour(5, 6)

    @pl.when(c == 0)
    def _():
        wait_recv(tab_copies)

    other = 1 - k
    arrived(3 + other)
    arrived(5 + other - 4 * zl)
    arrived(1 + other + 4 * zl)
    arrived(7 - 7 * other)

    for r in range(SOURCES):
        slot = jnp.minimum(lax.rem(blocks[0, r] - 2 * m + 3 + N_DOM, N_DOM), 7)
        h, l = split(slots[slot])
        xs[0:FLUX, r * CELLS : (r + 1) * CELLS] = h
        xs[FLUX : 2 * FLUX, r * CELLS : (r + 1) * CELLS] = l

    def remap(g, carry):
        cols = pl.ds(pl.multiple_of(g * GROUP, GROUP), GROUP)
        a = dot(xs[...], ph[:, cols])
        value = a[0:FLUX] + a[FLUX : 2 * FLUX] + dot(xs[0:FLUX, :], pl_[:, cols])
        imported[:, cols] = value
        exported[:, cols] = value
        h, l = split(value)
        mid = pl.ds(pl.multiple_of((g + 2) * GROUP, GROUP), GROUP)
        ie[0:FLUX, mid] = h
        ie[FLUX : 2 * FLUX, mid] = l
        return carry

    slot_copies[0].wait_send()
    slot_copies[1].wait_send()
    level = 2 * c

    def forced(number, source, offset, g):
        mid = pl.ds(pl.multiple_of((g + offset) * GROUP, GROUP), GROUP)
        a = dot(dst[number], source[0:FLUX, mid])
        return a[0:NV] + a[NV : 2 * NV] + dot(dst[number, 0:NV, :], source[FLUX : 2 * FLUX, mid])

    def first_forcing(g, carry):
        cols = pl.ds(pl.multiple_of(g * GROUP, GROUP), GROUP)
        out[:, cols] = states[level, :, cols] + forced(0, ie, 2, g)
        return carry

    lax.fori_loop(0, 2, remap, 0)

    def send_imported(half):
        if half == 0:
            return send(exported.at[:, pl.ds(0, 512)], far_r, i_send.at[0], i_recv.at[0], left)
        return send(exported.at[:, pl.ds(512, 512)], far_l, i_send.at[1], i_recv.at[1], right)

    @pl.when(c == 1)
    def _():
        send_imported(0)

    lax.fori_loop(2, 4, remap, 0)

    @pl.when(c == 1)
    def _():
        send_imported(1)

    lax.fori_loop(0, 4, first_forcing, 0)

    @pl.when(c == 1)
    def _():
        for side in range(2):
            piece = pl.ds(512 * side, 512)
            copy = pltpu.make_async_remote_copy(
                src_ref=exported.at[:, piece], dst_ref=(far_r, far_l)[side], send_sem=i_send.at[side],
                recv_sem=i_recv.at[side], device_id=(left, right)[side], device_id_type=MESH,
            )
            copy.wait()
        for side, start in ((far_l, 0), (far_r, 6 * GROUP)):
            h, l = split(side[...])
            ie[0:FLUX, pl.ds(start, 512)] = h
            ie[FLUX : 2 * FLUX, pl.ds(start, 512)] = l

        def apply(source, matrix, g):
            window = pl.ds(pl.multiple_of(g * GROUP, GROUP), WINDOW)
            a = dot(source[:, window], nh[matrix])
            return a[0:FLUX] + a[FLUX : 2 * FLUX] + dot(source[0:FLUX, window], nl[matrix])

        def once(g, carry):
            h, l = split(apply(ie, g, g))
            cols = pl.ds(pl.multiple_of(g * GROUP, GROUP), GROUP)
            ine[0:FLUX, cols] = h
            ine[FLUX : 2 * FLUX, cols] = l
            return carry

        lax.fori_loop(0, 6, once, 0)

        def twice(g, carry):
            value = apply(ine, g + 1, g)
            h, l = split(value)
            a = dot(dst[2], h)
            cols = pl.ds(pl.multiple_of(g * GROUP, GROUP), GROUP)
            out[:, cols] = out[:, cols] + forced(1, ine, 1, g) + (
                a[0:NV] + a[NV : 2 * NV] + dot(dst[2, 0:NV, :], l)
            )
            return carry

        lax.fori_loop(0, 4, twice, 0)

    wait_send(slot_copies[2:])
    wait_send(halo0)
    wait_send(tab_copies)


def per_device(prognostic, neighbours, diffusivity, vertical, export_map, import_map,
               ocean_mask, source_blocks, remap_index, remap_weights):
    vmem = pl.BlockSpec(memory_space=pltpu.VMEM)
    smem = pl.BlockSpec(memory_space=pltpu.SMEM)
    dma = pltpu.SemaphoreType.DMA
    stepped, imported = pl.pallas_call(
        kernel,
        out_shape=(
            jax.ShapeDtypeStruct((NV, CELLS), f32),
            jax.ShapeDtypeStruct((FLUX, CELLS), f32),
        ),
        in_specs=[vmem] * 7 + [smem] + [vmem] * 2,
        out_specs=(vmem, vmem),
        scratch_shapes=[
            pltpu.VMEM((FLUX, CELLS), f32),
            pltpu.VMEM((8, FLUX, CELLS), f32),
            pltpu.VMEM((SOURCES * CELLS, CELLS), bf16),
            pltpu.VMEM((SOURCES * CELLS, CELLS), bf16),
            pltpu.VMEM((TAPS, CELLS), f32),
            pltpu.VMEM((16 * TAPS, CELLS), bf16),
            pltpu.VMEM((16 * TAPS, CELLS), bf16),
            pltpu.VMEM((6, 16, GROUP), f32),
            pltpu.VMEM((6, WINDOW, GROUP), bf16),
            pltpu.VMEM((6, WINDOW, GROUP), bf16),
            pltpu.VMEM((3, NV, HALO), f32),
            pltpu.VMEM((3, NV, HALO), f32),
            pltpu.VMEM((2 * NV, 6 * GROUP), bf16),
            pltpu.VMEM((3, NV, CELLS), f32),
            pltpu.VMEM((2 * NV, NV), bf16),
            pltpu.VMEM((3, 2 * NV, FLUX), bf16),
            pltpu.VMEM((2 * FLUX, SOURCES * CELLS), bf16),
            pltpu.VMEM((2 * FLUX, 8 * GROUP), bf16),
            pltpu.VMEM((2 * FLUX, 6 * GROUP), bf16),
            pltpu.VMEM((FLUX, 512), f32),
            pltpu.VMEM((FLUX, 512), f32),
            dma((8,)), dma((8,)), dma((6,)), dma((6,)), dma((2,)), dma((2,)), dma((2,)), dma((2,)),
        ],
        compiler_params=pltpu.CompilerParams(
            collective_id=1, has_side_effects=True, vmem_limit_bytes=56 * 2**20
        ),
        name="coupled_interval",
    )(
        prognostic[0], neighbours[0], diffusivity[0], vertical[0], export_map[0], import_map[0],
        ocean_mask, source_blocks[0], remap_index[0], remap_weights[0],
    )
    return stepped[None], imported[None]


def solution(mesh):
    return jax.shard_map(
        per_device,
        mesh=mesh,
        in_specs=(
            P("comp", None, "dom"),
            P("comp", None, "dom"),
            P("comp", None, "dom"),
            P("comp", None, None),
            P("comp", None, None),
            P("comp", None, None),
            P("comp", "dom"),
            P("comp", "dom", None),
            P("comp", None, "dom"),
            P("comp", None, "dom"),
        ),
        out_specs=(P("comp", None, "dom"), P("comp", None, "dom")),
        check_vma=False,
    )
```

```python
import jax
import jax.numpy as jnp
from jax import lax
from jax.experimental import pallas as pl
from jax.experimental.pallas import tpu as pltpu
from jax.sharding import PartitionSpec as P

CELLS = 1024
NBR = 6
FLUX = 48
TAPS = 16
SOURCES = 3
NV = 144
HALO = 256
N_DOM = 64
TILE = 128
ROWS = 256
GROUP = 256
WINDOW = GROUP + 2 * HALO
MESH = pl.DeviceIdType.MESH
f32 = jnp.float32
bf16 = jnp.bfloat16


def split(x):
    high = x.astype(bf16)
    return high, (x - high.astype(f32)).astype(bf16)


def dot(a, b):
    return jnp.dot(a, b, preferred_element_type=f32)


def dot3(a, b):
    ah, al = split(a)
    bh, bl = split(b)
    return dot(ah, bh) + dot(al, bh) + dot(ah, bl)


def row_iota(n):
    return lax.broadcasted_iota(jnp.int32, (16, TILE), 0).astype(f32)


def spread(places, highs, lows, rows):
    base = row_iota(rows)
    count = rows // 16
    keys = [(base + 16.0 * r).astype(bf16) for r in range(count)]
    high = [jnp.zeros((16, TILE), bf16)] * count
    low = [jnp.zeros((16, TILE), bf16)] * count
    for place, h, l in zip(places, highs, lows):
        for r in range(count):
            hit = place == keys[r]
            high[r] = jnp.where(hit, h, high[r])
            low[r] = jnp.where(hit, l, low[r])
    return high, low


def kernel(
    prog, nbr, diff, vert, emap, imap, mask, blocks, ridx, rw,
    out, imported,
    exported, slots, ph, pl_, place, wh, wl,
    table, nh, nl, halo_l, halo_r, ub, states, vst, dst,
    xs, ie, ine, fh, fl, far_l, far_r,
    slot_send, slot_recv, uh_send, uh_recv, tab_send, tab_recv, i_send, i_recv,
):
    c = lax.axis_index("comp")
    d = lax.axis_index("dom")
    k = lax.rem(d, 2)
    m = d // 2
    zl = lax.rem(m, 2)
    left = (c, lax.rem(d + N_DOM - 1, N_DOM))
    right = (c, lax.rem(d + 1, N_DOM))
    sibling = (c, d + 1 - 2 * k)
    along_z = (c, 2 * (m + 1 - 2 * zl) + k)
    beside = (1 - c, 2 * (m + 1 - 2 * zl) + k)
    up = lax.rem(d + 4, N_DOM)
    down = lax.rem(d + N_DOM - 4, N_DOM)

    barrier = pltpu.get_barrier_semaphore()
    for peer in (left, right, along_z, beside, (c, up), (c, down)):
        pl.semaphore_signal(barrier, inc=1, device_id=peer, device_id_type=MESH)

    emap_h, emap_l = split(emap[...])
    est = jnp.concatenate([emap_h, emap_l], axis=0)
    for g in range(4):
        cols = pl.ds(g * GROUP, GROUP)
        uh, ul = split(prog[:, cols])
        ub[0:NV, pl.ds((g + 1) * GROUP, GROUP)] = uh
        ub[NV : 2 * NV, pl.ds((g + 1) * GROUP, GROUP)] = ul
        both = dot(est, uh)
        exported[:, cols] = mask[:, cols].astype(f32) * (
            both[0:FLUX] + both[FLUX : 2 * FLUX] + dot(emap_h, ul)
        )

    def send(src, dst, s_sem, r_sem, peer):
        copy = pltpu.make_async_remote_copy(
            src_ref=src, dst_ref=dst, send_sem=s_sem, recv_sem=r_sem,
            device_id=peer, device_id_type=MESH,
        )
        copy.start()
        return copy

    def to_slot(src, slot, number, peer):
        return send(src, slots.at[slot], slot_send.at[number], slot_recv.at[slot], peer)

    def pass_on(slot, target, number, peer):
        slot_copies.append(to_slot(slots.at[slot], target, number, peer))

    def arrived(slot):
        pltpu.make_async_remote_copy(
            src_ref=slots.at[slot], dst_ref=slots.at[slot], send_sem=slot_send.at[0],
            recv_sem=slot_recv.at[slot], device_id=sibling, device_id_type=MESH,
        ).wait_recv()

    own = 3 + k
    from_z = 5 + k - 4 * zl
    from_y = 1 + k + 4 * zl
    edge = 7 - 7 * k

    pl.semaphore_wait(barrier, 6)
    slot_copies = [to_slot(exported, from_y, 0, beside)]

    def send_halo(source, level):
        return [
            send(source.at[:, pl.ds(0, HALO)], halo_r.at[level], uh_send.at[2 * level],
                 uh_recv.at[2 * level], left),
            send(source.at[:, pl.ds(CELLS - HALO, HALO)], halo_l.at[level], uh_send.at[2 * level + 1],
                 uh_recv.at[2 * level + 1], right),
        ]

    halo0 = send_halo(prog, 0)

    places = []
    weights = []
    total = jnp.zeros((1, CELLS), f32)
    for s in range(NBR):
        e = nbr[s]
        w = diff[s]
        total = total + w
        double = jnp.zeros((1, CELLS), jnp.bool_)
        for t in range(s):
            same = places[t] == e
            weights[t] = weights[t] + jnp.where(same, w, 0.0)
            double = jnp.logical_or(double, same)
        places.append(jnp.where(double, -4096, e))
        weights.append(w)
    for g in range(4):
        cols = slice(g * GROUP, (g + 1) * GROUP)
        for s in range(NBR):
            table[g + 1, s : s + 1, :] = (places[s][:, cols] - g * GROUP).astype(f32)
            table[g + 1, 8 + s : 9 + s, :] = weights[s][:, cols]
        table[g + 1, 6:7, :] = (lax.broadcasted_iota(jnp.int32, (1, GROUP), 1) + HALO).astype(f32)
        table[g + 1, 14:15, :] = 1.0 - total[:, cols]
    tab_copies = [
        send(table.at[4], table.at[0], tab_send.at[0], tab_recv.at[0], right),
        send(table.at[1], table.at[5], tab_send.at[1], tab_recv.at[1], left),
    ]

    idx = ridx[...]
    w = rw[...]
    tap = lax.broadcasted_iota(jnp.int32, (TAPS, CELLS), 0)
    total_w = w
    double = tap < 0
    for s in range(1, TAPS):
        same = idx == pltpu.roll(idx, s, 0)
        total_w = total_w + jnp.where(same, pltpu.roll(w, s, 0), 0.0)
        double = jnp.logical_or(double, jnp.logical_and(same, tap >= s))
    place[...] = jnp.where(double, -4096, idx).astype(f32)
    for t in range(TAPS):
        h, l = split(jnp.broadcast_to(total_w[t : t + 1, :], (16, CELLS)))
        wh[16 * t : 16 * t + 16, :] = h
        wl[16 * t : 16 * t + 16, :] = l

    def build_remap(first, last):
        def chunk(i, carry):
            row = (i // 8) * ROWS
            cols = pl.ds(pl.multiple_of(lax.rem(i, 8) * TILE, TILE), TILE)
            base = row.astype(f32)
            at = [
                (jnp.broadcast_to(place[t : t + 1, cols], (16, TILE)) - base).astype(bf16)
                for t in range(TAPS)
            ]
            high, low = spread(
                at,
                [wh[16 * t : 16 * t + 16, cols] for t in range(TAPS)],
                [wl[16 * t : 16 * t + 16, cols] for t in range(TAPS)],
                ROWS,
            )
            for r in range(ROWS // 16):
                rows = pl.ds(pl.multiple_of(row + 16 * r, 16), 16)
                ph[rows, cols] = high[r]
                pl_[rows, cols] = low[r]
            return carry

        lax.fori_loop(first, last, chunk, 0)

    def build_neighbour(first, last):
        def chunk(i, carry):
            g = i // 6
            half = lax.rem(i, 6) // 3
            row = lax.rem(i, 3) * ROWS
            cols = pl.ds(pl.multiple_of(half * TILE, TILE), TILE)
            base = row.astype(f32)
            at, highs, lows = [], [], []
            for s in range(NBR + 1):
                at.append((jnp.broadcast_to(table[g, s : s + 1, cols], (16, TILE)) - base).astype(bf16))
                h, l = split(jnp.broadcast_to(table[g, 8 + s : 9 + s, cols], (16, TILE)))
                highs.append(h)
                lows.append(l)
            high, low = spread(at, highs, lows, ROWS)
            for r in range(ROWS // 16):
                rows = pl.ds(pl.multiple_of(row + 16 * r, 16), 16)
                nh[g, rows, cols] = high[r]
                nl[g, rows, cols] = low[r]
            return carry

        lax.fori_loop(6 * first, 6 * last, chunk, 0)

    vh, vl = split(vert[...])
    vst[0:NV, :] = vh
    vst[NV : 2 * NV, :] = vl

    def advance(level):
        for side, start in ((halo_l, 0), (halo_r, 5 * GROUP)):
            h, l = split(side[level])
            ub[0:NV, pl.ds(start, GROUP)] = h
            ub[NV : 2 * NV, pl.ds(start, GROUP)] = l

        def group(g, carry):
            window = pl.ds(pl.multiple_of(g * GROUP, GROUP), WINDOW)
            mid = pl.ds(pl.multiple_of((g + 1) * GROUP, GROUP), GROUP)
            a = dot(ub[:, window], nh[g + 1])
            b = dot(vst[...], ub[0:NV, mid])
            total = a[0:NV] + a[NV : 2 * NV] + dot(ub[0:NV, window], nl[g + 1])
            total = total + (b[0:NV] + b[NV : 2 * NV] + dot(vst[0:NV, :], ub[NV : 2 * NV, mid]))
            states[level, :, pl.ds(pl.multiple_of(g * GROUP, GROUP), GROUP)] = total
            return carry

        lax.fori_loop(0, 4, group, 0, unroll=True)

    def refill(level):
        def group(g, carry):
            mid = pl.ds(pl.multiple_of((g + 1) * GROUP, GROUP), GROUP)
            h, l = split(states[level, :, pl.ds(pl.multiple_of(g * GROUP, GROUP), GROUP)])
            ub[0:NV, mid] = h
            ub[NV : 2 * NV, mid] = l
            return carry

        lax.fori_loop(0, 4, group, 0, unroll=True)

    def wait_recv(copies):
        for copy in copies:
            copy.wait_recv()

    def wait_send(copies):
        for copy in copies:
            copy.wait_send()

    build_neighbour(1, 5)
    build_remap(0, 16)

    arrived(from_z)
    pass_on(from_z, own, 1, along_z)
    pass_on(from_z, from_y, 2, (c, lax.select(zl == 0, up, down)))
    pass_on(from_z, from_z, 3, sibling)

    wait_recv(halo0)
    advance(0)

    @pl.when(c == 1)
    def _():
        wait_send(send_halo(states.at[0], 1))

    build_remap(16, 40)

    arrived(own)
    pass_on(own, edge, 4, (c, lax.select(k == 1, up, down)))
    pass_on(own, own, 5, sibling)
    arrived(from_y)
    pass_on(from_y, from_y, 6, sibling)

    build_remap(40, 64)

    arrived(edge)
    pass_on(edge, edge, 7, sibling)

    def halo_arrived(level):
        for side in range(2):
            pltpu.make_async_remote_copy(
                src_ref=halo_l.at[level], dst_ref=(halo_r, halo_l)[side].at[level],
                send_sem=uh_send.at[2 * level + side], recv_sem=uh_recv.at[2 * level + side],
                device_id=left, device_id_type=MESH,
            ).wait_recv()

    @pl.when(c == 1)
    def _():
        refill(0)
        halo_arrived(1)
        advance(1)
        wait_send(send_halo(states.at[1], 2))

    build_remap(64, 96)

    m0 = imap[...].T

    def coefficients(values):
        for number, value in enumerate(values):
            h, l = split(value)
            cols = slice(FLUX * number, FLUX * (number + 1))
            dst[0:NV, cols] = h
            dst[NV : 2 * NV, cols] = l

    @pl.when(c == 0)
    def _():
        coefficients((m0, jnp.zeros_like(m0), jnp.zeros_like(m0)))
        fh[FLUX : 3 * FLUX, :] = jnp.zeros((2 * FLUX, CELLS), bf16)
        fl[FLUX : 3 * FLUX, :] = jnp.zeros((2 * FLUX, CELLS), bf16)

    @pl.when(c == 1)
    def _():
        v = vert[...]
        vm = dot3(v, m0)
        coefficients((m0 + vm + dot3(v, vm), m0 + 2.0 * vm, m0))

    other = 1 - k
    arrived(3 + other)
    arrived(5 + other - 4 * zl)
    arrived(1 + other + 4 * zl)
    arrived(7 - 7 * other)

    for r in range(SOURCES):
        slot = jnp.minimum(lax.rem(blocks[0, r] - 2 * m + 3 + N_DOM, N_DOM), 7)
        h, l = split(slots[slot])
        xs[0:FLUX, r * CELLS : (r + 1) * CELLS] = h
        xs[FLUX : 2 * FLUX, r * CELLS : (r + 1) * CELLS] = l

    def remap(g):
        cols = slice(g * GROUP, (g + 1) * GROUP)
        a = dot(xs[...], ph[:, cols])
        value = a[0:FLUX] + a[FLUX : 2 * FLUX] + dot(xs[0:FLUX, :], pl_[:, cols])
        imported[:, cols] = value
        exported[:, cols] = value
        h, l = split(value)
        mid = slice((g + 2) * GROUP, (g + 3) * GROUP)
        ie[0:FLUX, mid] = h
        ie[FLUX : 2 * FLUX, mid] = l
        fh[0:FLUX, cols] = h
        fl[0:FLUX, cols] = l

    slot_copies[0].wait_send()

    def imported_copy(side):
        return pltpu.make_async_remote_copy(
            src_ref=exported.at[:, pl.ds(512 * side, 512)], dst_ref=(far_r, far_l)[side],
            send_sem=i_send.at[side], recv_sem=i_recv.at[side],
            device_id=(left, right)[side], device_id_type=MESH,
        )

    for side in range(2):
        remap(2 * side)
        remap(2 * side + 1)

        @pl.when(c == 1)
        def _():
            imported_copy(side).start()

    def apply(source, matrix, g):
        window = slice(g * GROUP, g * GROUP + WINDOW)
        a = dot(source[:, window], nh[matrix])
        return a[0:FLUX] + a[FLUX : 2 * FLUX] + dot(source[0:FLUX, window], nl[matrix])

    def once(g):
        h, l = split(apply(ie, g, g))
        cols = slice(g * GROUP, (g + 1) * GROUP)
        ine[0:FLUX, cols] = h
        ine[FLUX : 2 * FLUX, cols] = l
        if 1 <= g < 5:
            mid = slice((g - 1) * GROUP, g * GROUP)
            fh[FLUX : 2 * FLUX, mid] = h
            fl[FLUX : 2 * FLUX, mid] = l

    @pl.when(c == 1)
    def _():
        refill(1)
        halo_arrived(2)
        advance(2)
        wait_recv(tab_copies)
        build_neighbour(0, 1)
        build_neighbour(5, 6)
        once(2)
        once(3)
        for side in range(2):
            imported_copy(side).wait()
        for side, start in ((far_l, 0), (far_r, 6 * GROUP)):
            h, l = split(side[...])
            ie[0:FLUX, start : start + 512] = h
            ie[FLUX : 2 * FLUX, start : start + 512] = l
        for g in (0, 1, 4, 5):
            once(g)
        for g in range(4):
            h, l = split(apply(ine, g + 1, g))
            cols = slice(g * GROUP, (g + 1) * GROUP)
            fh[2 * FLUX : 3 * FLUX, cols] = h
            fl[2 * FLUX : 3 * FLUX, cols] = l

    @pl.when(c == 0)
    def _():
        wait_recv(tab_copies)

    level = 2 * c
    for g in range(4):
        cols = slice(g * GROUP, (g + 1) * GROUP)
        a = dot(dst[...], fh[:, cols])
        out[:, cols] = states[level, :, cols] + (
            a[0:NV] + a[NV : 2 * NV] + dot(dst[0:NV, :], fl[:, cols])
        )

    wait_send(slot_copies[1:])
    wait_send(halo0)
    wait_send(tab_copies)


def per_device(prognostic, neighbours, diffusivity, vertical, export_map, import_map,
               ocean_mask, source_blocks, remap_index, remap_weights):
    vmem = pl.BlockSpec(memory_space=pltpu.VMEM)
    smem = pl.BlockSpec(memory_space=pltpu.SMEM)
    dma = pltpu.SemaphoreType.DMA
    stepped, imported = pl.pallas_call(
        kernel,
        out_shape=(
            jax.ShapeDtypeStruct((NV, CELLS), f32),
            jax.ShapeDtypeStruct((FLUX, CELLS), f32),
        ),
        in_specs=[vmem] * 7 + [smem] + [vmem] * 2,
        out_specs=(vmem, vmem),
        scratch_shapes=[
            pltpu.VMEM((FLUX, CELLS), f32),
            pltpu.VMEM((8, FLUX, CELLS), f32),
            pltpu.VMEM((SOURCES * CELLS, CELLS), bf16),
            pltpu.VMEM((SOURCES * CELLS, CELLS), bf16),
            pltpu.VMEM((TAPS, CELLS), f32),
            pltpu.VMEM((16 * TAPS, CELLS), bf16),
            pltpu.VMEM((16 * TAPS, CELLS), bf16),
            pltpu.VMEM((6, 16, GROUP), f32),
            pltpu.VMEM((6, WINDOW, GROUP), bf16),
            pltpu.VMEM((6, WINDOW, GROUP), bf16),
            pltpu.VMEM((3, NV, HALO), f32),
            pltpu.VMEM((3, NV, HALO), f32),
            pltpu.VMEM((2 * NV, 6 * GROUP), bf16),
            pltpu.VMEM((3, NV, CELLS), f32),
            pltpu.VMEM((2 * NV, NV), bf16),
            pltpu.VMEM((2 * NV, 3 * FLUX), bf16),
            pltpu.VMEM((2 * FLUX, SOURCES * CELLS), bf16),
            pltpu.VMEM((2 * FLUX, 8 * GROUP), bf16),
            pltpu.VMEM((2 * FLUX, 6 * GROUP), bf16),
            pltpu.VMEM((3 * FLUX, CELLS), bf16),
            pltpu.VMEM((3 * FLUX, CELLS), bf16),
            pltpu.VMEM((FLUX, 512), f32),
            pltpu.VMEM((FLUX, 512), f32),
            dma((8,)), dma((8,)), dma((6,)), dma((6,)), dma((2,)), dma((2,)), dma((2,)), dma((2,)),
        ],
        compiler_params=pltpu.CompilerParams(
            collective_id=1, has_side_effects=True, vmem_limit_bytes=56 * 2**20
        ),
        name="coupled_interval",
    )(
        prognostic[0], jnp.transpose(neighbours, (1, 0, 2)), jnp.transpose(diffusivity, (1, 0, 2)),
        vertical[0], export_map[0], jnp.transpose(import_map[0]),
        ocean_mask, source_blocks[0], remap_index[0], remap_weights[0],
    )
    return stepped[None], imported[None]


def solution(mesh):
    return jax.shard_map(
        per_device,
        mesh=mesh,
        in_specs=(
            P("comp", None, "dom"),
            P("comp", None, "dom"),
            P("comp", None, "dom"),
            P("comp", None, None),
            P("comp", None, None),
            P("comp", None, None),
            P("comp", "dom"),
            P("comp", "dom", None),
            P("comp", None, "dom"),
            P("comp", None, "dom"),
        ),
        out_specs=(P("comp", None, "dom"), P("comp", None, "dom")),
        check_vma=False,
    )
```

```python
import jax
import jax.numpy as jnp
from jax import lax
from jax.experimental import pallas as pl
from jax.experimental.pallas import tpu as pltpu
from jax.sharding import PartitionSpec as P

CELLS = 1024
NBR = 6
FLUX = 48
TAPS = 16
SOURCES = 3
NV = 144
HALO = 256
N_DOM = 64
TILE = 128
ROWS = 256
GROUP = 256
WINDOW = GROUP + 2 * HALO
PIECE = 24
PLAN = (12, 20, 20, 36, 48, 64, 72, 76)
MESH = pl.DeviceIdType.MESH
f32 = jnp.float32
bf16 = jnp.bfloat16


def split(x):
    high = x.astype(bf16)
    return high, (x - high.astype(f32)).astype(bf16)


def dot(a, b):
    return jnp.dot(a, b, preferred_element_type=f32)


def dot3(a, b):
    ah, al = split(a)
    bh, bl = split(b)
    return dot(ah, bh) + dot(al, bh) + dot(ah, bl)


def row_iota(n):
    return lax.broadcasted_iota(jnp.int32, (16, TILE), 0).astype(f32)


def spread(places, highs, lows, rows):
    base = row_iota(rows)
    count = rows // 16
    keys = [(base + 16.0 * r).astype(bf16) for r in range(count)]
    high = [jnp.zeros((16, TILE), bf16)] * count
    low = [jnp.zeros((16, TILE), bf16)] * count
    for place, h, l in zip(places, highs, lows):
        for r in range(count):
            hit = place == keys[r]
            high[r] = jnp.where(hit, h, high[r])
            low[r] = jnp.where(hit, l, low[r])
    return high, low


def kernel(
    prog, nbr, diff, vert, emap, imap, mask, blocks, ridx, rw,
    out, imported,
    exported, slots, ph, pl_, place, wh, wl,
    table, nh, nl, halo_l, halo_r, ub, states, vst, dst,
    xs, ie, ine, fh, fl, far_l, far_r,
    slot_send, slot_recv, uh_send, uh_recv, tab_send, tab_recv, i_send, i_recv,
):
    c = lax.axis_index("comp")
    d = lax.axis_index("dom")
    k = lax.rem(d, 2)
    m = d // 2
    zl = lax.rem(m, 2)
    left = (c, lax.rem(d + N_DOM - 1, N_DOM))
    right = (c, lax.rem(d + 1, N_DOM))
    sibling = (c, d + 1 - 2 * k)
    along_z = (c, 2 * (m + 1 - 2 * zl) + k)
    beside = (1 - c, 2 * (m + 1 - 2 * zl) + k)
    up = lax.rem(d + 4, N_DOM)
    down = lax.rem(d + N_DOM - 4, N_DOM)

    barrier = pltpu.get_barrier_semaphore()
    for peer in (left, right, along_z, beside, (c, up), (c, down)):
        pl.semaphore_signal(barrier, inc=1, device_id=peer, device_id_type=MESH)

    emap_h, emap_l = split(emap[...])
    est = jnp.concatenate([emap_h, emap_l], axis=0)
    for g in range(4):
        cols = pl.ds(g * GROUP, GROUP)
        uh, ul = split(prog[:, cols])
        ub[0:NV, pl.ds((g + 1) * GROUP, GROUP)] = uh
        ub[NV : 2 * NV, pl.ds((g + 1) * GROUP, GROUP)] = ul
        both = dot(est, uh)
        exported[:, cols] = mask[:, cols].astype(f32) * (
            both[0:FLUX] + both[FLUX : 2 * FLUX] + dot(emap_h, ul)
        )

    def send(src, dst, s_sem, r_sem, peer):
        copy = pltpu.make_async_remote_copy(
            src_ref=src, dst_ref=dst, send_sem=s_sem, recv_sem=r_sem,
            device_id=peer, device_id_type=MESH,
        )
        copy.start()
        return copy

    slot_copies = []

    def to_slot(src, slot, number, peer, piece):
        copy = send(
            src, slots.at[slot, pl.ds(PIECE * piece, PIECE)], slot_send.at[number, piece],
            slot_recv.at[slot, piece], peer,
        )
        slot_copies.append(copy)

    def pass_on(slot, target, number, peer, piece):
        to_slot(slots.at[slot, pl.ds(PIECE * piece, PIECE)], target, number, peer, piece)

    def arrived(slot, piece):
        rows = slots.at[slot, pl.ds(PIECE * piece, PIECE)]
        pltpu.make_async_remote_copy(
            src_ref=rows, dst_ref=rows, send_sem=slot_send.at[0, piece],
            recv_sem=slot_recv.at[slot, piece], device_id=sibling, device_id_type=MESH,
        ).wait_recv()

    own = 3 + k
    from_z = 5 + k - 4 * zl
    from_y = 1 + k + 4 * zl
    edge = 7 - 7 * k

    pl.semaphore_wait(barrier, 6)
    for piece in range(2):
        to_slot(exported.at[pl.ds(PIECE * piece, PIECE)], from_y, 0, beside, piece)

    def send_halo(source, level):
        return [
            send(source.at[:, pl.ds(0, HALO)], halo_r.at[level], uh_send.at[2 * level],
                 uh_recv.at[2 * level], left),
            send(source.at[:, pl.ds(CELLS - HALO, HALO)], halo_l.at[level], uh_send.at[2 * level + 1],
                 uh_recv.at[2 * level + 1], right),
        ]

    halo0 = send_halo(prog, 0)

    places = []
    weights = []
    total = jnp.zeros((1, CELLS), f32)
    for s in range(NBR):
        e = nbr[s]
        w = diff[s]
        total = total + w
        double = jnp.zeros((1, CELLS), jnp.bool_)
        for t in range(s):
            same = places[t] == e
            weights[t] = weights[t] + jnp.where(same, w, 0.0)
            double = jnp.logical_or(double, same)
        places.append(jnp.where(double, -4096, e))
        weights.append(w)
    for g in range(4):
        cols = slice(g * GROUP, (g + 1) * GROUP)
        for s in range(NBR):
            table[g + 1, s : s + 1, :] = (places[s][:, cols] - g * GROUP).astype(f32)
            table[g + 1, 8 + s : 9 + s, :] = weights[s][:, cols]
        table[g + 1, 6:7, :] = (lax.broadcasted_iota(jnp.int32, (1, GROUP), 1) + HALO).astype(f32)
        table[g + 1, 14:15, :] = 1.0 - total[:, cols]
    tab_copies = [
        send(table.at[4], table.at[0], tab_send.at[0], tab_recv.at[0], right),
        send(table.at[1], table.at[5], tab_send.at[1], tab_recv.at[1], left),
    ]

    idx = ridx[...]
    w = rw[...]
    tap = lax.broadcasted_iota(jnp.int32, (TAPS, CELLS), 0)
    total_w = w
    double = tap < 0
    for s in range(1, TAPS):
        same = idx == pltpu.roll(idx, s, 0)
        total_w = total_w + jnp.where(same, pltpu.roll(w, s, 0), 0.0)
        double = jnp.logical_or(double, jnp.logical_and(same, tap >= s))
    place[...] = jnp.where(double, -4096, idx).astype(f32)
    for t in range(TAPS):
        h, l = split(jnp.broadcast_to(total_w[t : t + 1, :], (16, CELLS)))
        wh[16 * t : 16 * t + 16, :] = h
        wl[16 * t : 16 * t + 16, :] = l

    def remap_chunk(i):
        row = (i // 8) * ROWS
        cols = pl.ds(pl.multiple_of(lax.rem(i, 8) * TILE, TILE), TILE)
        base = row.astype(f32)
        at = [
            (jnp.broadcast_to(place[t : t + 1, cols], (16, TILE)) - base).astype(bf16)
            for t in range(TAPS)
        ]
        high, low = spread(
            at,
            [wh[16 * t : 16 * t + 16, cols] for t in range(TAPS)],
            [wl[16 * t : 16 * t + 16, cols] for t in range(TAPS)],
            ROWS,
        )
        for r in range(ROWS // 16):
            rows = pl.ds(pl.multiple_of(row + 16 * r, 16), 16)
            ph[rows, cols] = high[r]
            pl_[rows, cols] = low[r]

    def build_remap(first, last):
        def chunk(i, carry):
            remap_chunk(i)
            return carry

        lax.fori_loop(first, last, chunk, 0)

    def build_neighbour(first, last):
        def chunk(i, carry):
            g = i // 6
            half = lax.rem(i, 6) // 3
            row = lax.rem(i, 3) * ROWS
            cols = pl.ds(pl.multiple_of(half * TILE, TILE), TILE)
            base = row.astype(f32)
            at, highs, lows = [], [], []
            for s in range(NBR + 1):
                at.append((jnp.broadcast_to(table[g, s : s + 1, cols], (16, TILE)) - base).astype(bf16))
                h, l = split(jnp.broadcast_to(table[g, 8 + s : 9 + s, cols], (16, TILE)))
                highs.append(h)
                lows.append(l)
            high, low = spread(at, highs, lows, ROWS)
            for r in range(ROWS // 16):
                rows = pl.ds(pl.multiple_of(row + 16 * r, 16), 16)
                nh[g, rows, cols] = high[r]
                nl[g, rows, cols] = low[r]
            return carry

        lax.fori_loop(6 * first, 6 * last, chunk, 0)

    vh, vl = split(vert[...])
    vst[0:NV, :] = vh
    vst[NV : 2 * NV, :] = vl

    def advance(level, first=0, beside_it=0):
        for side, start in ((halo_l, 0), (halo_r, 5 * GROUP)):
            h, l = split(side[level])
            ub[0:NV, pl.ds(start, GROUP)] = h
            ub[NV : 2 * NV, pl.ds(start, GROUP)] = l

        def group(g, carry):
            window = pl.ds(pl.multiple_of(g * GROUP, GROUP), WINDOW)
            mid = pl.ds(pl.multiple_of((g + 1) * GROUP, GROUP), GROUP)
            a = dot(ub[:, window], nh[g + 1])
            b = dot(vst[...], ub[0:NV, mid])
            total = a[0:NV] + a[NV : 2 * NV] + dot(ub[0:NV, window], nl[g + 1])
            total = total + (b[0:NV] + b[NV : 2 * NV] + dot(vst[0:NV, :], ub[NV : 2 * NV, mid]))
            states[level, :, pl.ds(pl.multiple_of(g * GROUP, GROUP), GROUP)] = total
            for j in range(beside_it):
                remap_chunk(first + beside_it * g + j)
            return carry

        lax.fori_loop(0, 4, group, 0, unroll=beside_it == 0)

    def refill(level):
        def group(g, carry):
            mid = pl.ds(pl.multiple_of((g + 1) * GROUP, GROUP), GROUP)
            h, l = split(states[level, :, pl.ds(pl.multiple_of(g * GROUP, GROUP), GROUP)])
            ub[0:NV, mid] = h
            ub[NV : 2 * NV, mid] = l
            return carry

        lax.fori_loop(0, 4, group, 0, unroll=True)

    def wait_recv(copies):
        for copy in copies:
            copy.wait_recv()

    def wait_send(copies):
        for copy in copies:
            copy.wait_send()

    p = PLAN
    build_neighbour(1, 5)
    build_remap(0, p[0])

    def crossed(piece):
        arrived(from_z, piece)
        pass_on(from_z, own, 1, along_z, piece)
        pass_on(from_z, from_y, 2, (c, lax.select(zl == 0, up, down)), piece)
        pass_on(from_z, from_z, 3, sibling, piece)

    def spread_along_y(piece):
        arrived(own, piece)
        pass_on(own, edge, 4, (c, lax.select(k == 1, up, down)), piece)
        pass_on(own, own, 5, sibling, piece)
        arrived(from_y, piece)
        pass_on(from_y, from_y, 6, sibling, piece)

    def shared(piece):
        arrived(edge, piece)
        pass_on(edge, edge, 7, sibling, piece)

    crossed(0)
    build_remap(p[0], p[1])
    crossed(1)
    wait_recv(halo0)
    build_remap(p[1], p[2])
    advance(0, p[2], 4)

    @pl.when(c == 1)
    def _():
        send_halo(states.at[0], 1)

    build_remap(p[2] + 16, p[3])
    spread_along_y(0)
    build_remap(p[3], p[4])
    spread_along_y(1)
    build_remap(p[4], p[5])
    shared(0)
    build_remap(p[5], p[6])
    shared(1)
    build_remap(p[6], p[7])

    def halo_copy(level, side):
        return pltpu.make_async_remote_copy(
            src_ref=states.at[level - 1, :, pl.ds((CELLS - HALO) * side, HALO)],
            dst_ref=(halo_r, halo_l)[side].at[level],
            send_sem=uh_send.at[2 * level + side], recv_sem=uh_recv.at[2 * level + side],
            device_id=(left, right)[side], device_id_type=MESH,
        )

    def halo_arrived(level):
        for side in range(2):
            halo_copy(level, side).wait_recv()

    @pl.when(c == 0)
    def _():
        build_remap(p[7], p[7] + 16)

    @pl.when(c == 1)
    def _():
        refill(0)
        halo_arrived(1)
        advance(1, p[7], 4)
        send_halo(states.at[1], 2)

    build_remap(p[7] + 16, 96)

    m0 = imap[...].T

    def coefficients(values):
        for number, value in enumerate(values):
            h, l = split(value)
            cols = slice(FLUX * number, FLUX * (number + 1))
            dst[0:NV, cols] = h
            dst[NV : 2 * NV, cols] = l

    @pl.when(c == 0)
    def _():
        coefficients((m0, jnp.zeros_like(m0), jnp.zeros_like(m0)))
        fh[FLUX : 3 * FLUX, :] = jnp.zeros((2 * FLUX, CELLS), bf16)
        fl[FLUX : 3 * FLUX, :] = jnp.zeros((2 * FLUX, CELLS), bf16)

    @pl.when(c == 1)
    def _():
        v = vert[...]
        vm = dot3(v, m0)
        coefficients((m0 + vm + dot3(v, vm), m0 + 2.0 * vm, m0))

    other = 1 - k
    for piece in range(2):
        arrived(3 + other, piece)
        arrived(5 + other - 4 * zl, piece)
        arrived(1 + other + 4 * zl, piece)
        arrived(7 - 7 * other, piece)

    for r in range(SOURCES):
        slot = jnp.minimum(lax.rem(blocks[0, r] - 2 * m + 3 + N_DOM, N_DOM), 7)
        h, l = split(slots[slot])
        xs[0:FLUX, r * CELLS : (r + 1) * CELLS] = h
        xs[FLUX : 2 * FLUX, r * CELLS : (r + 1) * CELLS] = l

    def remap(g):
        cols = slice(g * GROUP, (g + 1) * GROUP)
        a = dot(xs[...], ph[:, cols])
        value = a[0:FLUX] + a[FLUX : 2 * FLUX] + dot(xs[0:FLUX, :], pl_[:, cols])
        imported[:, cols] = value
        exported[:, cols] = value
        h, l = split(value)
        mid = slice((g + 2) * GROUP, (g + 3) * GROUP)
        ie[0:FLUX, mid] = h
        ie[FLUX : 2 * FLUX, mid] = l
        fh[0:FLUX, cols] = h
        fl[0:FLUX, cols] = l

    wait_send(slot_copies[0:2])

    def imported_copy(side):
        return pltpu.make_async_remote_copy(
            src_ref=exported.at[:, pl.ds(512 * side, 512)], dst_ref=(far_r, far_l)[side],
            send_sem=i_send.at[side], recv_sem=i_recv.at[side],
            device_id=(left, right)[side], device_id_type=MESH,
        )

    for side in range(2):
        remap(2 * side)
        remap(2 * side + 1)

        @pl.when(c == 1)
        def _():
            imported_copy(side).start()

    def apply(source, matrix, g):
        window = slice(g * GROUP, g * GROUP + WINDOW)
        a = dot(source[:, window], nh[matrix])
        return a[0:FLUX] + a[FLUX : 2 * FLUX] + dot(source[0:FLUX, window], nl[matrix])

    def once(g):
        h, l = split(apply(ie, g, g))
        cols = slice(g * GROUP, (g + 1) * GROUP)
        ine[0:FLUX, cols] = h
        ine[FLUX : 2 * FLUX, cols] = l
        if 1 <= g < 5:
            mid = slice((g - 1) * GROUP, g * GROUP)
            fh[FLUX : 2 * FLUX, mid] = h
            fl[FLUX : 2 * FLUX, mid] = l

    @pl.when(c == 1)
    def _():
        refill(1)
        halo_arrived(2)
        advance(2)
        wait_recv(tab_copies)
        build_neighbour(0, 1)
        build_neighbour(5, 6)
        once(2)
        once(3)
        for side in range(2):
            imported_copy(side).wait_recv()
        for side, start in ((far_l, 0), (far_r, 6 * GROUP)):
            h, l = split(side[...])
            ie[0:FLUX, start : start + 512] = h
            ie[FLUX : 2 * FLUX, start : start + 512] = l
        for g in (0, 1, 4, 5):
            once(g)
        for g in range(4):
            h, l = split(apply(ine, g + 1, g))
            cols = slice(g * GROUP, (g + 1) * GROUP)
            fh[2 * FLUX : 3 * FLUX, cols] = h
            fl[2 * FLUX : 3 * FLUX, cols] = l
        for side in range(2):
            halo_copy(1, side).wait_send()
            halo_copy(2, side).wait_send()
            imported_copy(side).wait_send()

    @pl.when(c == 0)
    def _():
        wait_recv(tab_copies)

    level = 2 * c
    for g in range(4):
        cols = slice(g * GROUP, (g + 1) * GROUP)
        a = dot(dst[...], fh[:, cols])
        out[:, cols] = states[level, :, cols] + (
            a[0:NV] + a[NV : 2 * NV] + dot(dst[0:NV, :], fl[:, cols])
        )

    wait_send(slot_copies[2:])
    wait_send(halo0)
    wait_send(tab_copies)


def per_device(prognostic, neighbours, diffusivity, vertical, export_map, import_map,
               ocean_mask, source_blocks, remap_index, remap_weights):
    vmem = pl.BlockSpec(memory_space=pltpu.VMEM)
    smem = pl.BlockSpec(memory_space=pltpu.SMEM)
    dma = pltpu.SemaphoreType.DMA
    stepped, imported = pl.pallas_call(
        kernel,
        out_shape=(
            jax.ShapeDtypeStruct((NV, CELLS), f32),
            jax.ShapeDtypeStruct((FLUX, CELLS), f32),
        ),
        in_specs=[vmem] * 7 + [smem] + [vmem] * 2,
        out_specs=(vmem, vmem),
        scratch_shapes=[
            pltpu.VMEM((FLUX, CELLS), f32),
            pltpu.VMEM((8, FLUX, CELLS), f32),
            pltpu.VMEM((SOURCES * CELLS, CELLS), bf16),
            pltpu.VMEM((SOURCES * CELLS, CELLS), bf16),
            pltpu.VMEM((TAPS, CELLS), f32),
            pltpu.VMEM((16 * TAPS, CELLS), bf16),
            pltpu.VMEM((16 * TAPS, CELLS), bf16),
            pltpu.VMEM((6, 16, GROUP), f32),
            pltpu.VMEM((6, WINDOW, GROUP), bf16),
            pltpu.VMEM((6, WINDOW, GROUP), bf16),
            pltpu.VMEM((3, NV, HALO), f32),
            pltpu.VMEM((3, NV, HALO), f32),
            pltpu.VMEM((2 * NV, 6 * GROUP), bf16),
            pltpu.VMEM((3, NV, CELLS), f32),
            pltpu.VMEM((2 * NV, NV), bf16),
            pltpu.VMEM((2 * NV, 3 * FLUX), bf16),
            pltpu.VMEM((2 * FLUX, SOURCES * CELLS), bf16),
            pltpu.VMEM((2 * FLUX, 8 * GROUP), bf16),
            pltpu.VMEM((2 * FLUX, 6 * GROUP), bf16),
            pltpu.VMEM((3 * FLUX, CELLS), bf16),
            pltpu.VMEM((3 * FLUX, CELLS), bf16),
            pltpu.VMEM((FLUX, 512), f32),
            pltpu.VMEM((FLUX, 512), f32),
            dma((8, 2)), dma((8, 2)), dma((6,)), dma((6,)), dma((2,)), dma((2,)), dma((2,)), dma((2,)),
        ],
        compiler_params=pltpu.CompilerParams(
            collective_id=1, has_side_effects=True, vmem_limit_bytes=56 * 2**20
        ),
        name="coupled_interval",
    )(
        prognostic[0], jnp.transpose(neighbours, (1, 0, 2)), jnp.transpose(diffusivity, (1, 0, 2)),
        vertical[0], export_map[0], jnp.transpose(import_map[0]),
        ocean_mask, source_blocks[0], remap_index[0], remap_weights[0],
    )
    return stepped[None], imported[None]


def solution(mesh):
    return jax.shard_map(
        per_device,
        mesh=mesh,
        in_specs=(
            P("comp", None, "dom"),
            P("comp", None, "dom"),
            P("comp", None, "dom"),
            P("comp", None, None),
            P("comp", None, None),
            P("comp", None, None),
            P("comp", "dom"),
            P("comp", "dom", None),
            P("comp", None, "dom"),
            P("comp", None, "dom"),
        ),
        out_specs=(P("comp", None, "dom"), P("comp", None, "dom")),
        check_vma=False,
    )
```

```python
import jax
import jax.numpy as jnp
from jax import lax
from jax.experimental import pallas as pl
from jax.experimental.pallas import tpu as pltpu
from jax.sharding import PartitionSpec as P

CELLS = 1024
NBR = 6
FLUX = 48
TAPS = 16
SOURCES = 3
NV = 144
HALO = 256
N_DOM = 64
TILE = 128
ROWS = 256
GROUP = 256
WINDOW = GROUP + 2 * HALO
PIECE = 24
PIECES = 24
UNROLL = 4
PLAN = (12, 20, 24, 40, 52, 64, 72)
MESH = pl.DeviceIdType.MESH
f32 = jnp.float32
bf16 = jnp.bfloat16


def split(x):
    high = x.astype(bf16)
    return high, (x - high.astype(f32)).astype(bf16)


def dot(a, b):
    return jnp.dot(a, b, preferred_element_type=f32)


def dot3(a, b):
    ah, al = split(a)
    bh, bl = split(b)
    return dot(ah, bh) + dot(al, bh) + dot(ah, bl)


def row_iota():
    return lax.broadcasted_iota(jnp.int32, (16, TILE), 0).astype(f32)


def spread(places, highs, lows, rows):
    count = rows // 16
    high = [jnp.zeros((16, TILE), bf16)] * count
    low = [jnp.zeros((16, TILE), bf16)] * count
    for place, h, l in zip(places, highs, lows):
        for r in range(count):
            hit = place == bf16(16 * r)
            high[r] = jnp.where(hit, h, high[r])
            low[r] = jnp.where(hit, l, low[r])
    return high, low


def kernel(
    prog_in, nbr_in, diff_in, vert_in, emap_in, imap_in, mask_in, blocks, ridx_in, rw_in,
    out, imported,
    prog, nbr, diff, vert, emap, imap, mask, ridx, rw,
    exported, slots, ph0, ph1, ph2, ph3, pl0, pl1, pl2, pl3, place, wh, wl,
    table, nh, nl, halo_l, halo_r, ub, states, vst, dst,
    xs, ie, ine, fh, fl, far_l, far_r,
    in_sem, slot_send, slot_recv, uh_send, uh_recv, tab_send, tab_recv, i_send, i_recv,
):
    ph = (ph0, ph1, ph2, ph3)
    pl_ = (pl0, pl1, pl2, pl3)
    c = lax.axis_index("comp")
    d = lax.axis_index("dom")
    k = lax.rem(d, 2)
    m = d // 2
    zl = lax.rem(m, 2)
    left = (c, lax.rem(d + N_DOM - 1, N_DOM))
    right = (c, lax.rem(d + 1, N_DOM))
    sibling = (c, d + 1 - 2 * k)
    along_z = (c, 2 * (m + 1 - 2 * zl) + k)
    beside = (1 - c, 2 * (m + 1 - 2 * zl) + k)
    up = lax.rem(d + 4, N_DOM)
    down = lax.rem(d + N_DOM - 4, N_DOM)

    barrier = pltpu.get_barrier_semaphore()
    for peer in (left, right, along_z, beside, (c, up), (c, down)):
        pl.semaphore_signal(barrier, inc=1, device_id=peer, device_id_type=MESH)

    inputs = [
        pltpu.make_async_copy(src, dst, in_sem.at[number])
        for number, (src, dst) in enumerate((
            (prog_in, prog), (emap_in, emap), (mask_in, mask), (nbr_in, nbr), (diff_in, diff),
            (ridx_in, ridx), (rw_in, rw), (vert_in, vert), (imap_in, imap),
        ))
    ]
    for copy in inputs:
        copy.start()
    for copy in inputs[0:3]:
        copy.wait()

    emap_h, emap_l = split(emap[...])
    est = jnp.concatenate([emap_h, emap_l], axis=0)
    for g in range(4):
        cols = pl.ds(g * GROUP, GROUP)
        uh, ul = split(prog[:, cols])
        ub[0:NV, pl.ds((g + 1) * GROUP, GROUP)] = uh
        ub[NV : 2 * NV, pl.ds((g + 1) * GROUP, GROUP)] = ul
        both = dot(est, uh)
        exported[:, cols] = mask[:, cols].astype(f32) * (
            both[0:FLUX] + both[FLUX : 2 * FLUX] + dot(emap_h, ul)
        )

    def send(src, dst, s_sem, r_sem, peer):
        copy = pltpu.make_async_remote_copy(
            src_ref=src, dst_ref=dst, send_sem=s_sem, recv_sem=r_sem,
            device_id=peer, device_id_type=MESH,
        )
        copy.start()
        return copy

    slot_copies = []

    def to_slot(src, slot, number, peer, piece):
        copy = send(
            src, slots.at[slot, pl.ds(PIECE * piece, PIECE)], slot_send.at[number, piece],
            slot_recv.at[slot, piece], peer,
        )
        slot_copies.append(copy)

    def pass_on(slot, target, number, peer, piece):
        to_slot(slots.at[slot, pl.ds(PIECE * piece, PIECE)], target, number, peer, piece)

    def arrived(slot, piece):
        rows = slots.at[slot, pl.ds(PIECE * piece, PIECE)]
        pltpu.make_async_remote_copy(
            src_ref=rows, dst_ref=rows, send_sem=slot_send.at[0, piece],
            recv_sem=slot_recv.at[slot, piece], device_id=sibling, device_id_type=MESH,
        ).wait_recv()

    own = 3 + k
    from_z = 5 + k - 4 * zl
    from_y = 1 + k + 4 * zl
    edge = 7 - 7 * k

    pl.semaphore_wait(barrier, 6)
    for piece in range(2):
        to_slot(exported.at[pl.ds(PIECE * piece, PIECE)], from_y, 0, beside, piece)

    def send_halo(source, level):
        return [
            send(source.at[:, pl.ds(0, HALO)], halo_r.at[level], uh_send.at[2 * level],
                 uh_recv.at[2 * level], left),
            send(source.at[:, pl.ds(CELLS - HALO, HALO)], halo_l.at[level], uh_send.at[2 * level + 1],
                 uh_recv.at[2 * level + 1], right),
        ]

    halo0 = send_halo(prog, 0)
    for copy in inputs[3:]:
        copy.wait()

    places = []
    weights = []
    total = jnp.zeros((1, CELLS), f32)
    for s in range(NBR):
        e = nbr[s]
        w = diff[s]
        total = total + w
        double = jnp.zeros((1, CELLS), jnp.bool_)
        for t in range(s):
            same = places[t] == e
            weights[t] = weights[t] + jnp.where(same, w, 0.0)
            double = jnp.logical_or(double, same)
        places.append(jnp.where(double, -4096, e))
        weights.append(w)
    for g in range(4):
        cols = slice(g * GROUP, (g + 1) * GROUP)
        for s in range(NBR):
            table[g + 1, s : s + 1, :] = (places[s][:, cols] - g * GROUP).astype(f32)
            table[g + 1, 8 + s : 9 + s, :] = weights[s][:, cols]
        table[g + 1, 6:7, :] = (lax.broadcasted_iota(jnp.int32, (1, GROUP), 1) + HALO).astype(f32)
        table[g + 1, 14:15, :] = 1.0 - total[:, cols]
    tab_copies = [
        send(table.at[4], table.at[0], tab_send.at[0], tab_recv.at[0], right),
        send(table.at[1], table.at[5], tab_send.at[1], tab_recv.at[1], left),
    ]

    idx = ridx[...]
    w = rw[...]
    tap = lax.broadcasted_iota(jnp.int32, (TAPS, CELLS), 0)
    total_w = w
    double = tap < 0
    for s in range(1, TAPS):
        same = idx == pltpu.roll(idx, s, 0)
        total_w = total_w + jnp.where(same, pltpu.roll(w, s, 0), 0.0)
        double = jnp.logical_or(double, jnp.logical_and(same, tap >= s))
    place[...] = jnp.where(double, -4096, idx).astype(f32)
    for t in range(TAPS):
        h, l = split(jnp.broadcast_to(total_w[t : t + 1, :], (16, CELLS)))
        wh[16 * t : 16 * t + 16, :] = h
        wl[16 * t : 16 * t + 16, :] = l

    def relative(row, base):
        return (jnp.broadcast_to(row, (16, TILE)) - base).astype(bf16) - row_iota().astype(bf16)

    def remap_chunk(i, group):
        i = i - PIECES * group
        half = i // (PIECES // 2)
        row = lax.rem(i, PIECES // 2) * ROWS
        cols = pl.ds(pl.multiple_of(half * TILE, TILE), TILE)
        wide = pl.ds(pl.multiple_of(group * GROUP + half * TILE, TILE), TILE)
        base = row.astype(f32)
        high, low = spread(
            [relative(place[t : t + 1, wide], base) for t in range(TAPS)],
            [wh[16 * t : 16 * t + 16, wide] for t in range(TAPS)],
            [wl[16 * t : 16 * t + 16, wide] for t in range(TAPS)],
            ROWS,
        )
        for r in range(ROWS // 16):
            rows = pl.ds(pl.multiple_of(row + 16 * r, 16), 16)
            ph[group][rows, cols] = high[r]
            pl_[group][rows, cols] = low[r]

    def build_remap(first, last):
        for group in range(4):
            def chunk(i, carry):
                for j in range(UNROLL):
                    remap_chunk(UNROLL * i + j, group)
                return carry

            low = max(first, PIECES * group)
            high = min(last, PIECES * (group + 1))
            if low < high:
                lax.fori_loop(low // UNROLL, high // UNROLL, chunk, 0)

    def build_neighbour(g):
        def part(half, carry):
            cols = pl.ds(pl.multiple_of(half * TILE, TILE), TILE)
            start = half * TILE
            base = start.astype(f32)
            split_weights = [
                split(jnp.broadcast_to(table[g, 8 + s : 9 + s, cols], (16, TILE)))
                for s in range(NBR + 1)
            ]
            for block in range(5):
                taps = NBR + 1 if block == 2 else NBR
                high, low = spread(
                    [relative(table[g, s : s + 1, cols], base + 128.0 * block) for s in range(taps)],
                    [split_weights[s][0] for s in range(taps)],
                    [split_weights[s][1] for s in range(taps)],
                    TILE,
                )
                for r in range(TILE // 16):
                    rows = pl.ds(pl.multiple_of(start + TILE * block + 16 * r, 16), 16)
                    nh[g, rows, cols] = high[r]
                    nl[g, rows, cols] = low[r]
            rest = pl.ds(pl.multiple_of((1 - half) * 5 * TILE, TILE), TILE)
            nh[g, rest, cols] = jnp.zeros((TILE, TILE), bf16)
            nl[g, rest, cols] = jnp.zeros((TILE, TILE), bf16)
            return carry

        lax.fori_loop(0, 2, part, 0)

    vh, vl = split(vert[...])
    vst[0:NV, :] = vh
    vst[NV : 2 * NV, :] = vl

    def advance(level, first=0, beside_it=0):
        for side, start in ((halo_l, 0), (halo_r, 5 * GROUP)):
            h, l = split(side[level])
            ub[0:NV, pl.ds(start, GROUP)] = h
            ub[NV : 2 * NV, pl.ds(start, GROUP)] = l

        def group(g, carry):
            window = pl.ds(pl.multiple_of(g * GROUP, GROUP), WINDOW)
            mid = pl.ds(pl.multiple_of((g + 1) * GROUP, GROUP), GROUP)
            a = dot(ub[:, window], nh[g + 1])
            b = dot(vst[...], ub[0:NV, mid])
            total = a[0:NV] + a[NV : 2 * NV] + dot(ub[0:NV, window], nl[g + 1])
            total = total + (b[0:NV] + b[NV : 2 * NV] + dot(vst[0:NV, :], ub[NV : 2 * NV, mid]))
            states[level, :, pl.ds(pl.multiple_of(g * GROUP, GROUP), GROUP)] = total
            for j in range(beside_it):
                remap_chunk(first + beside_it * g + j, first // PIECES)
            return carry

        lax.fori_loop(0, 4, group, 0, unroll=beside_it == 0)

    def refill(level):
        def group(g, carry):
            mid = pl.ds(pl.multiple_of((g + 1) * GROUP, GROUP), GROUP)
            h, l = split(states[level, :, pl.ds(pl.multiple_of(g * GROUP, GROUP), GROUP)])
            ub[0:NV, mid] = h
            ub[NV : 2 * NV, mid] = l
            return carry

        lax.fori_loop(0, 4, group, 0, unroll=True)

    def wait_recv(copies):
        for copy in copies:
            copy.wait_recv()

    def wait_send(copies):
        for copy in copies:
            copy.wait_send()

    p = PLAN
    for g in range(1, 5):
        build_neighbour(g)
    build_remap(0, p[0])

    def crossed(piece):
        arrived(from_z, piece)
        pass_on(from_z, own, 1, along_z, piece)
        pass_on(from_z, from_y, 2, (c, lax.select(zl == 0, up, down)), piece)
        pass_on(from_z, from_z, 3, sibling, piece)

    def spread_along_y(piece):
        arrived(own, piece)
        pass_on(own, edge, 4, (c, lax.select(k == 1, up, down)), piece)
        pass_on(own, own, 5, sibling, piece)
        arrived(from_y, piece)
        pass_on(from_y, from_y, 6, sibling, piece)

    def shared(piece):
        arrived(edge, piece)
        pass_on(edge, edge, 7, sibling, piece)

    crossed(0)
    build_remap(p[0], p[1])
    crossed(1)
    wait_recv(halo0)
    build_remap(p[1], p[2])
    advance(0, p[2], 4)

    @pl.when(c == 1)
    def _():
        send_halo(states.at[0], 1)

    build_remap(p[2] + 16, p[3])
    spread_along_y(0)
    build_remap(p[3], p[4])
    spread_along_y(1)
    build_remap(p[4], p[5])
    shared(0)
    build_remap(p[5], p[6])
    shared(1)

    def halo_copy(level, side):
        return pltpu.make_async_remote_copy(
            src_ref=states.at[level - 1, :, pl.ds((CELLS - HALO) * side, HALO)],
            dst_ref=(halo_r, halo_l)[side].at[level],
            send_sem=uh_send.at[2 * level + side], recv_sem=uh_recv.at[2 * level + side],
            device_id=(left, right)[side], device_id_type=MESH,
        )

    def halo_arrived(level):
        for side in range(2):
            halo_copy(level, side).wait_recv()

    @pl.when(c == 0)
    def _():
        build_remap(72, 84)

    @pl.when(c == 1)
    def _():
        refill(0)
        halo_arrived(1)
        advance(1, 72, 3)
        send_halo(states.at[1], 2)

    m0 = imap[...].T

    def coefficients(values):
        for number, value in enumerate(values):
            h, l = split(value)
            cols = slice(FLUX * number, FLUX * (number + 1))
            dst[0:NV, cols] = h
            dst[NV : 2 * NV, cols] = l

    other = 1 - k
    for piece in range(2):
        arrived(3 + other, piece)
        arrived(5 + other - 4 * zl, piece)
        arrived(1 + other + 4 * zl, piece)
        arrived(7 - 7 * other, piece)

    for r in range(SOURCES):
        slot = jnp.minimum(lax.rem(blocks[0, r] - 2 * m + 3 + N_DOM, N_DOM), 7)
        h, l = split(slots[slot])
        xs[0:FLUX, r * CELLS : (r + 1) * CELLS] = h
        xs[FLUX : 2 * FLUX, r * CELLS : (r + 1) * CELLS] = l

    wait_send(slot_copies[0:2])

    def remap_beside(g):
        cols = slice(g * GROUP, (g + 1) * GROUP)
        exported[:, cols] = jnp.zeros((FLUX, GROUP), f32)

        def step(j, carry):
            depth = pl.ds(pl.multiple_of(j * 768, 768), 768)
            a = dot(xs[:, depth], ph[g][depth, :])
            exported[:, cols] += a[0:FLUX] + a[FLUX : 2 * FLUX] + dot(xs[0:FLUX, depth], pl_[g][depth, :])
            remap_chunk(84 + 4 * g + j, 3)
            return carry

        lax.fori_loop(0, 4, step, 0)

    def remap_last():
        a = dot(xs[...], ph[3][...])
        exported[:, 3 * GROUP :] = a[0:FLUX] + a[FLUX : 2 * FLUX] + dot(xs[0:FLUX, :], pl_[3][...])

    def keep(g):
        cols = slice(g * GROUP, (g + 1) * GROUP)
        value = exported[:, cols]
        imported[:, cols] = value
        h, l = split(value)
        mid = slice((g + 2) * GROUP, (g + 3) * GROUP)
        ie[0:FLUX, mid] = h
        ie[FLUX : 2 * FLUX, mid] = l
        fh[0:FLUX, cols] = h
        fl[0:FLUX, cols] = l

    def imported_copy(g):
        side = g // 2
        cols = pl.ds(GROUP * g, GROUP)
        there = pl.ds(GROUP * (g - 2 * side), GROUP)
        return pltpu.make_async_remote_copy(
            src_ref=exported.at[:, cols], dst_ref=(far_r, far_l)[side].at[:, there],
            send_sem=i_send.at[g], recv_sem=i_recv.at[g],
            device_id=(left, right)[side], device_id_type=MESH,
        )

    def start_imported(g):
        @pl.when(c == 1)
        def _():
            imported_copy(g).start()

    for g in range(3):
        remap_beside(g)
        start_imported(g)
    remap_last()
    start_imported(3)
    for g in range(4):
        keep(g)

    def apply(source, matrix, g):
        window = slice(g * GROUP, g * GROUP + WINDOW)
        a = dot(source[:, window], nh[matrix])
        return a[0:FLUX] + a[FLUX : 2 * FLUX] + dot(source[0:FLUX, window], nl[matrix])

    def once(g):
        h, l = split(apply(ie, g, g))
        cols = slice(g * GROUP, (g + 1) * GROUP)
        ine[0:FLUX, cols] = h
        ine[FLUX : 2 * FLUX, cols] = l
        if 1 <= g < 5:
            mid = slice((g - 1) * GROUP, g * GROUP)
            fh[FLUX : 2 * FLUX, mid] = h
            fl[FLUX : 2 * FLUX, mid] = l

    @pl.when(c == 1)
    def _():
        refill(1)
        halo_arrived(2)
        advance(2)
        v = vert[...]
        vm = dot3(v, m0)
        coefficients((m0 + vm + dot3(v, vm), m0 + 2.0 * vm, m0))
        wait_recv(tab_copies)
        build_neighbour(0)
        build_neighbour(5)
        once(2)
        once(3)
        for g in range(4):
            imported_copy(g).wait_recv()
        for side, start in ((far_l, 0), (far_r, 6 * GROUP)):
            h, l = split(side[...])
            ie[0:FLUX, start : start + 512] = h
            ie[FLUX : 2 * FLUX, start : start + 512] = l
        for g in (0, 1, 4, 5):
            once(g)
        for g in range(4):
            h, l = split(apply(ine, g + 1, g))
            cols = slice(g * GROUP, (g + 1) * GROUP)
            fh[2 * FLUX : 3 * FLUX, cols] = h
            fl[2 * FLUX : 3 * FLUX, cols] = l
        for side in range(2):
            halo_copy(1, side).wait_send()
            halo_copy(2, side).wait_send()
        for g in range(4):
            imported_copy(g).wait_send()

    @pl.when(c == 0)
    def _():
        coefficients((m0, jnp.zeros_like(m0), jnp.zeros_like(m0)))
        fh[FLUX : 3 * FLUX, :] = jnp.zeros((2 * FLUX, CELLS), bf16)
        fl[FLUX : 3 * FLUX, :] = jnp.zeros((2 * FLUX, CELLS), bf16)
        wait_recv(tab_copies)

    level = 2 * c
    for g in range(4):
        cols = slice(g * GROUP, (g + 1) * GROUP)
        a = dot(dst[...], fh[:, cols])
        out[:, cols] = states[level, :, cols] + (
            a[0:NV] + a[NV : 2 * NV] + dot(dst[0:NV, :], fl[:, cols])
        )

    wait_send(slot_copies[2:])
    wait_send(halo0)
    wait_send(tab_copies)


def hand_over(stepped_in, imported_in, stepped, imported):
    stepped[...] = stepped_in[...]
    imported[...] = imported_in[...]


def per_device(prognostic, neighbours, diffusivity, vertical, export_map, import_map,
               ocean_mask, source_blocks, remap_index, remap_weights):
    vmem = pl.BlockSpec(memory_space=pltpu.VMEM)
    anywhere = pl.BlockSpec(memory_space=pl.ANY)
    smem = pl.BlockSpec(memory_space=pltpu.SMEM)
    dma = pltpu.SemaphoreType.DMA
    stepped, imported = pl.pallas_call(
        kernel,
        out_shape=(
            jax.ShapeDtypeStruct((NV, CELLS), f32),
            jax.ShapeDtypeStruct((FLUX, CELLS), f32),
        ),
        in_specs=[anywhere] * 7 + [smem] + [anywhere] * 2,
        out_specs=(vmem, vmem),
        scratch_shapes=[
            pltpu.VMEM((NV, CELLS), f32),
            pltpu.VMEM((NBR, 1, CELLS), jnp.int32),
            pltpu.VMEM((NBR, 1, CELLS), f32),
            pltpu.VMEM((NV, NV), f32),
            pltpu.VMEM((FLUX, NV), f32),
            pltpu.VMEM((FLUX, NV), f32),
            pltpu.VMEM((1, CELLS), jnp.int32),
            pltpu.VMEM((TAPS, CELLS), jnp.int32),
            pltpu.VMEM((TAPS, CELLS), f32),
            pltpu.VMEM((FLUX, CELLS), f32),
            pltpu.VMEM((8, FLUX, CELLS), f32),
            *[pltpu.VMEM((SOURCES * CELLS, GROUP), bf16)] * 8,
            pltpu.VMEM((TAPS, CELLS), f32),
            pltpu.VMEM((16 * TAPS, CELLS), bf16),
            pltpu.VMEM((16 * TAPS, CELLS), bf16),
            pltpu.VMEM((6, 16, GROUP), f32),
            pltpu.VMEM((6, WINDOW, GROUP), bf16),
            pltpu.VMEM((6, WINDOW, GROUP), bf16),
            pltpu.VMEM((3, NV, HALO), f32),
            pltpu.VMEM((3, NV, HALO), f32),
            pltpu.VMEM((2 * NV, 6 * GROUP), bf16),
            pltpu.VMEM((3, NV, CELLS), f32),
            pltpu.VMEM((2 * NV, NV), bf16),
            pltpu.VMEM((2 * NV, 3 * FLUX), bf16),
            pltpu.VMEM((2 * FLUX, SOURCES * CELLS), bf16),
            pltpu.VMEM((2 * FLUX, 8 * GROUP), bf16),
            pltpu.VMEM((2 * FLUX, 6 * GROUP), bf16),
            pltpu.VMEM((3 * FLUX, CELLS), bf16),
            pltpu.VMEM((3 * FLUX, CELLS), bf16),
            pltpu.VMEM((FLUX, 512), f32),
            pltpu.VMEM((FLUX, 512), f32),
            dma((9,)), dma((8, 2)), dma((8, 2)), dma((6,)), dma((6,)), dma((2,)), dma((2,)), dma((4,)), dma((4,)),
        ],
        compiler_params=pltpu.CompilerParams(
            collective_id=1, has_side_effects=True, vmem_limit_bytes=56 * 2**20
        ),
        name="coupled_interval",
    )(
        prognostic[0], jnp.transpose(neighbours, (1, 0, 2)), jnp.transpose(diffusivity, (1, 0, 2)),
        vertical[0], export_map[0], jnp.transpose(import_map[0]),
        ocean_mask, source_blocks[0], remap_index[0], remap_weights[0],
    )
    stepped, imported = pl.pallas_call(
        hand_over,
        out_shape=(
            jax.ShapeDtypeStruct((NV, CELLS), f32),
            jax.ShapeDtypeStruct((FLUX, CELLS), f32),
        ),
        name="hand_over",
    )(stepped, imported)
    return stepped[None], imported[None]


def solution(mesh):
    return jax.shard_map(
        per_device,
        mesh=mesh,
        in_specs=(
            P("comp", None, "dom"),
            P("comp", None, "dom"),
            P("comp", None, "dom"),
            P("comp", None, None),
            P("comp", None, None),
            P("comp", None, None),
            P("comp", "dom"),
            P("comp", "dom", None),
            P("comp", None, "dom"),
            P("comp", None, "dom"),
        ),
        out_specs=(P("comp", None, "dom"), P("comp", None, "dom")),
        check_vma=False,
    )
```

```python
import jax
import jax.numpy as jnp
from jax import lax
from jax.experimental import pallas as pl
from jax.experimental.pallas import tpu as pltpu
from jax.sharding import PartitionSpec as P

CELLS = 1024
NBR = 6
FLUX = 48
TAPS = 16
SOURCES = 3
NV = 144
HALO = 256
N_DOM = 64
TILE = 128
ROWS = 256
GROUP = 256
WINDOW = GROUP + 2 * HALO
PIECE = 24
PIECES = 24
UNROLL = 4
PLAN = (12, 20, 24, 40, 52, 64, 72)
MESH = pl.DeviceIdType.MESH
f32 = jnp.float32
bf16 = jnp.bfloat16


def split(x):
    high = x.astype(bf16)
    return high, (x - high.astype(f32)).astype(bf16)


def dot(a, b):
    return jnp.dot(a, b, preferred_element_type=f32)


def dot3(a, b):
    ah, al = split(a)
    bh, bl = split(b)
    return dot(ah, bh) + dot(al, bh) + dot(ah, bl)


def row_iota():
    return lax.broadcasted_iota(jnp.int32, (16, TILE), 0).astype(f32)


def spread(places, highs, lows, rows):
    count = rows // 16
    high = [jnp.zeros((16, TILE), bf16)] * count
    low = [jnp.zeros((16, TILE), bf16)] * count
    for place, h, l in zip(places, highs, lows):
        for r in range(count):
            hit = place == bf16(16 * r)
            high[r] = jnp.where(hit, h, high[r])
            low[r] = jnp.where(hit, l, low[r])
    return high, low


def kernel(
    prog_in, nbr_in, diff_in, vert_in, emap_in, imap_in, mask_in, blocks, ridx_in, rw_in,
    out, imported,
    prog, nbr, diff, vert, emap, imap, mask, ridx, rw,
    exported, slots, ph0, ph1, ph2, ph3, pl0, pl1, pl2, pl3, place, wh, wl,
    table, nh, nl, wide_l, wide_r, halo_l, halo_r, ub, states, vst, dst,
    xs, ie, ine, fh, fl, far_l, far_r,
    in_sem, slot_send, slot_recv, uh_send, uh_recv, tab_send, tab_recv, i_send, i_recv,
):
    ph = (ph0, ph1, ph2, ph3)
    pl_ = (pl0, pl1, pl2, pl3)
    c = lax.axis_index("comp")
    d = lax.axis_index("dom")
    k = lax.rem(d, 2)
    m = d // 2
    zl = lax.rem(m, 2)
    left = (c, lax.rem(d + N_DOM - 1, N_DOM))
    right = (c, lax.rem(d + 1, N_DOM))
    sibling = (c, d + 1 - 2 * k)
    along_z = (c, 2 * (m + 1 - 2 * zl) + k)
    beside = (1 - c, 2 * (m + 1 - 2 * zl) + k)
    up = lax.rem(d + 4, N_DOM)
    down = lax.rem(d + N_DOM - 4, N_DOM)

    barrier = pltpu.get_barrier_semaphore()
    for peer in (left, right, along_z, beside, (c, up), (c, down)):
        pl.semaphore_signal(barrier, inc=1, device_id=peer, device_id_type=MESH)

    inputs = [
        pltpu.make_async_copy(src, dst, in_sem.at[number])
        for number, (src, dst) in enumerate((
            (prog_in, prog), (emap_in, emap), (mask_in, mask), (nbr_in, nbr), (diff_in, diff),
            (ridx_in, ridx), (rw_in, rw), (vert_in, vert), (imap_in, imap),
        ))
    ]
    for copy in inputs:
        copy.start()
    for copy in inputs[0:3]:
        copy.wait()

    emap_h, emap_l = split(emap[...])
    est = jnp.concatenate([emap_h, emap_l], axis=0)
    for g in range(4):
        cols = pl.ds(g * GROUP, GROUP)
        uh, ul = split(prog[:, cols])
        ub[0:NV, pl.ds((g + 2) * GROUP, GROUP)] = uh
        ub[NV : 2 * NV, pl.ds((g + 2) * GROUP, GROUP)] = ul
        both = dot(est, uh)
        exported[:, cols] = mask[:, cols].astype(f32) * (
            both[0:FLUX] + both[FLUX : 2 * FLUX] + dot(emap_h, ul)
        )

    def send(src, dst, s_sem, r_sem, peer):
        copy = pltpu.make_async_remote_copy(
            src_ref=src, dst_ref=dst, send_sem=s_sem, recv_sem=r_sem,
            device_id=peer, device_id_type=MESH,
        )
        copy.start()
        return copy

    slot_copies = []

    def to_slot(src, slot, number, peer, piece):
        copy = send(
            src, slots.at[slot, pl.ds(PIECE * piece, PIECE)], slot_send.at[number, piece],
            slot_recv.at[slot, piece], peer,
        )
        slot_copies.append(copy)

    def pass_on(slot, target, number, peer, piece):
        to_slot(slots.at[slot, pl.ds(PIECE * piece, PIECE)], target, number, peer, piece)

    def arrived(slot, piece):
        rows = slots.at[slot, pl.ds(PIECE * piece, PIECE)]
        pltpu.make_async_remote_copy(
            src_ref=rows, dst_ref=rows, send_sem=slot_send.at[0, piece],
            recv_sem=slot_recv.at[slot, piece], device_id=sibling, device_id_type=MESH,
        ).wait_recv()

    own = 3 + k
    from_z = 5 + k - 4 * zl
    from_y = 1 + k + 4 * zl
    edge = 7 - 7 * k

    pl.semaphore_wait(barrier, 6)
    for piece in range(2):
        to_slot(exported.at[pl.ds(PIECE * piece, PIECE)], from_y, 0, beside, piece)

    halo0 = [
        send(prog.at[:, pl.ds(0, 2 * HALO)], wide_r, uh_send.at[0], uh_recv.at[0], left),
        send(prog.at[:, pl.ds(CELLS - 2 * HALO, 2 * HALO)], wide_l, uh_send.at[1], uh_recv.at[1], right),
    ]
    for copy in inputs[3:]:
        copy.wait()

    places = []
    weights = []
    total = jnp.zeros((1, CELLS), f32)
    for s in range(NBR):
        e = nbr[s]
        w = diff[s]
        total = total + w
        double = jnp.zeros((1, CELLS), jnp.bool_)
        for t in range(s):
            same = places[t] == e
            weights[t] = weights[t] + jnp.where(same, w, 0.0)
            double = jnp.logical_or(double, same)
        places.append(jnp.where(double, -4096, e))
        weights.append(w)
    for g in range(4):
        cols = slice(g * GROUP, (g + 1) * GROUP)
        for s in range(NBR):
            table[g + 1, s : s + 1, :] = (places[s][:, cols] - g * GROUP).astype(f32)
            table[g + 1, 8 + s : 9 + s, :] = weights[s][:, cols]
        table[g + 1, 6:7, :] = (lax.broadcasted_iota(jnp.int32, (1, GROUP), 1) + HALO).astype(f32)
        table[g + 1, 14:15, :] = 1.0 - total[:, cols]
    tab_copies = [
        send(table.at[4], table.at[0], tab_send.at[0], tab_recv.at[0], right),
        send(table.at[1], table.at[5], tab_send.at[1], tab_recv.at[1], left),
    ]

    idx = ridx[...]
    w = rw[...]
    tap = lax.broadcasted_iota(jnp.int32, (TAPS, CELLS), 0)
    total_w = w
    double = tap < 0
    for s in range(1, TAPS):
        same = idx == pltpu.roll(idx, s, 0)
        total_w = total_w + jnp.where(same, pltpu.roll(w, s, 0), 0.0)
        double = jnp.logical_or(double, jnp.logical_and(same, tap >= s))
    place[...] = jnp.where(double, -4096, idx).astype(f32)
    for t in range(TAPS):
        h, l = split(jnp.broadcast_to(total_w[t : t + 1, :], (16, CELLS)))
        wh[16 * t : 16 * t + 16, :] = h
        wl[16 * t : 16 * t + 16, :] = l

    def relative(row, base):
        return (jnp.broadcast_to(row, (16, TILE)) - base).astype(bf16) - row_iota().astype(bf16)

    def remap_chunk(i, group):
        i = i - PIECES * group
        half = i // (PIECES // 2)
        row = lax.rem(i, PIECES // 2) * ROWS
        cols = pl.ds(pl.multiple_of(half * TILE, TILE), TILE)
        wide = pl.ds(pl.multiple_of(group * GROUP + half * TILE, TILE), TILE)
        base = row.astype(f32)
        high, low = spread(
            [relative(place[t : t + 1, wide], base) for t in range(TAPS)],
            [wh[16 * t : 16 * t + 16, wide] for t in range(TAPS)],
            [wl[16 * t : 16 * t + 16, wide] for t in range(TAPS)],
            ROWS,
        )
        for r in range(ROWS // 16):
            rows = pl.ds(pl.multiple_of(row + 16 * r, 16), 16)
            ph[group][rows, cols] = high[r]
            pl_[group][rows, cols] = low[r]

    def build_remap(first, last):
        for group in range(4):
            def chunk(i, carry):
                for j in range(UNROLL):
                    remap_chunk(UNROLL * i + j, group)
                return carry

            low = max(first, PIECES * group)
            high = min(last, PIECES * (group + 1))
            if low < high:
                lax.fori_loop(low // UNROLL, high // UNROLL, chunk, 0)

    def build_neighbour(g):
        def part(half, carry):
            cols = pl.ds(pl.multiple_of(half * TILE, TILE), TILE)
            start = half * TILE
            base = start.astype(f32)
            split_weights = [
                split(jnp.broadcast_to(table[g, 8 + s : 9 + s, cols], (16, TILE)))
                for s in range(NBR + 1)
            ]
            for block in range(5):
                taps = NBR + 1 if block == 2 else NBR
                high, low = spread(
                    [relative(table[g, s : s + 1, cols], base + 128.0 * block) for s in range(taps)],
                    [split_weights[s][0] for s in range(taps)],
                    [split_weights[s][1] for s in range(taps)],
                    TILE,
                )
                for r in range(TILE // 16):
                    rows = pl.ds(pl.multiple_of(start + TILE * block + 16 * r, 16), 16)
                    nh[g, rows, cols] = high[r]
                    nl[g, rows, cols] = low[r]
            rest = pl.ds(pl.multiple_of((1 - half) * 5 * TILE, TILE), TILE)
            nh[g, rest, cols] = jnp.zeros((TILE, TILE), bf16)
            nl[g, rest, cols] = jnp.zeros((TILE, TILE), bf16)
            return carry

        lax.fori_loop(0, 2, part, 0)

    vh, vl = split(vert[...])
    vst[0:NV, :] = vh
    vst[NV : 2 * NV, :] = vl

    def fill(side, start, width):
        h, l = split(side[...])
        ub[0:NV, pl.ds(start, width)] = h
        ub[NV : 2 * NV, pl.ds(start, width)] = l

    def advance(level, groups, first=0, beside_it=0):
        start, stop = groups

        def group(g, carry):
            cols = pl.ds(pl.multiple_of(g * GROUP, GROUP), GROUP)
            window = pl.ds(pl.multiple_of(g * GROUP, GROUP), WINDOW)
            mid = pl.ds(pl.multiple_of((g + 1) * GROUP, GROUP), GROUP)
            a = dot(ub[:, window], nh[g])
            b = dot(vst[...], ub[0:NV, mid])
            total = a[0:NV] + a[NV : 2 * NV] + dot(ub[0:NV, window], nl[g])
            total = total + (b[0:NV] + b[NV : 2 * NV] + dot(vst[0:NV, :], ub[NV : 2 * NV, mid]))
            states[level, :, cols] = total
            for j in range(beside_it):
                remap_chunk(first + beside_it * (g - start) + j, first // PIECES)
            return carry

        lax.fori_loop(start, stop, group, 0, unroll=beside_it == 0)

    def refill(level, groups):
        def group(g, carry):
            mid = pl.ds(pl.multiple_of((g + 1) * GROUP, GROUP), GROUP)
            h, l = split(states[level, :, pl.ds(pl.multiple_of(g * GROUP, GROUP), GROUP)])
            ub[0:NV, mid] = h
            ub[NV : 2 * NV, mid] = l
            return carry

        lax.fori_loop(*groups, group, 0, unroll=True)

    def wait_recv(copies):
        for copy in copies:
            copy.wait_recv()

    def wait_send(copies):
        for copy in copies:
            copy.wait_send()

    p = PLAN
    for g in range(1, 5):
        build_neighbour(g)
    build_remap(0, p[0])

    def crossed(piece):
        arrived(from_z, piece)
        pass_on(from_z, own, 1, along_z, piece)
        pass_on(from_z, from_y, 2, (c, lax.select(zl == 0, up, down)), piece)
        pass_on(from_z, from_z, 3, sibling, piece)

    def spread_along_y(piece):
        arrived(own, piece)
        pass_on(own, edge, 4, (c, lax.select(k == 1, up, down)), piece)
        pass_on(own, own, 5, sibling, piece)
        arrived(from_y, piece)
        pass_on(from_y, from_y, 6, sibling, piece)

    def shared(piece):
        arrived(edge, piece)
        pass_on(edge, edge, 7, sibling, piece)

    crossed(0)
    build_remap(p[0], p[1])
    crossed(1)
    wait_recv(tab_copies)
    build_neighbour(0)
    build_neighbour(5)
    wait_recv(halo0)
    fill(wide_l, 0, 2 * HALO)
    fill(wide_r, 6 * GROUP, 2 * HALO)
    build_remap(p[1], p[2])
    advance(0, (0, 6), p[2], 2)

    build_remap(p[2] + 12, p[3])
    spread_along_y(0)
    build_remap(p[3], p[4])
    spread_along_y(1)
    build_remap(p[4], p[5])
    shared(0)
    build_remap(p[5], p[6])
    shared(1)

    def halo_copy(side):
        return pltpu.make_async_remote_copy(
            src_ref=states.at[1, :, pl.ds(GROUP + (CELLS - HALO) * side, HALO)],
            dst_ref=(halo_r, halo_l)[side], send_sem=uh_send.at[2 + side], recv_sem=uh_recv.at[2 + side],
            device_id=(left, right)[side], device_id_type=MESH,
        )

    @pl.when(c == 0)
    def _():
        build_remap(72, 84)

    @pl.when(c == 1)
    def _():
        refill(0, (0, 6))
        advance(1, (1, 5), 72, 3)
        for side in range(2):
            halo_copy(side).start()

    m0 = imap[...].T

    def coefficients(values):
        for number, value in enumerate(values):
            h, l = split(value)
            cols = slice(FLUX * number, FLUX * (number + 1))
            dst[0:NV, cols] = h
            dst[NV : 2 * NV, cols] = l

    other = 1 - k
    for piece in range(2):
        arrived(3 + other, piece)
        arrived(5 + other - 4 * zl, piece)
        arrived(1 + other + 4 * zl, piece)
        arrived(7 - 7 * other, piece)

    for r in range(SOURCES):
        slot = jnp.minimum(lax.rem(blocks[0, r] - 2 * m + 3 + N_DOM, N_DOM), 7)
        h, l = split(slots[slot])
        xs[0:FLUX, r * CELLS : (r + 1) * CELLS] = h
        xs[FLUX : 2 * FLUX, r * CELLS : (r + 1) * CELLS] = l

    wait_send(slot_copies[0:2])

    def remap_beside(g):
        cols = slice(g * GROUP, (g + 1) * GROUP)
        exported[:, cols] = jnp.zeros((FLUX, GROUP), f32)

        def step(j, carry):
            depth = pl.ds(pl.multiple_of(j * 768, 768), 768)
            a = dot(xs[:, depth], ph[g][depth, :])
            exported[:, cols] += a[0:FLUX] + a[FLUX : 2 * FLUX] + dot(xs[0:FLUX, depth], pl_[g][depth, :])
            remap_chunk(84 + 4 * g + j, 3)
            return carry

        lax.fori_loop(0, 4, step, 0)

    def remap_last():
        a = dot(xs[...], ph[3][...])
        exported[:, 3 * GROUP :] = a[0:FLUX] + a[FLUX : 2 * FLUX] + dot(xs[0:FLUX, :], pl_[3][...])

    def keep(g):
        cols = slice(g * GROUP, (g + 1) * GROUP)
        value = exported[:, cols]
        imported[:, cols] = value
        h, l = split(value)
        mid = slice((g + 2) * GROUP, (g + 3) * GROUP)
        ie[0:FLUX, mid] = h
        ie[FLUX : 2 * FLUX, mid] = l
        fh[0:FLUX, cols] = h
        fl[0:FLUX, cols] = l

    def imported_copy(g):
        side = g // 2
        cols = pl.ds(GROUP * g, GROUP)
        there = pl.ds(GROUP * (g - 2 * side), GROUP)
        return pltpu.make_async_remote_copy(
            src_ref=exported.at[:, cols], dst_ref=(far_r, far_l)[side].at[:, there],
            send_sem=i_send.at[g], recv_sem=i_recv.at[g],
            device_id=(left, right)[side], device_id_type=MESH,
        )

    def start_imported(g):
        @pl.when(c == 1)
        def _():
            imported_copy(g).start()

    for g in range(3):
        remap_beside(g)
        start_imported(g)
    remap_last()
    start_imported(3)
    for g in range(4):
        keep(g)

    def apply(source, matrix, g):
        window = slice(g * GROUP, g * GROUP + WINDOW)
        a = dot(source[:, window], nh[matrix])
        return a[0:FLUX] + a[FLUX : 2 * FLUX] + dot(source[0:FLUX, window], nl[matrix])

    def once(g):
        h, l = split(apply(ie, g, g))
        cols = slice(g * GROUP, (g + 1) * GROUP)
        ine[0:FLUX, cols] = h
        ine[FLUX : 2 * FLUX, cols] = l
        if 1 <= g < 5:
            mid = slice((g - 1) * GROUP, g * GROUP)
            fh[FLUX : 2 * FLUX, mid] = h
            fl[FLUX : 2 * FLUX, mid] = l

    @pl.when(c == 1)
    def _():
        v = vert[...]
        vm = dot3(v, m0)
        coefficients((m0 + vm + dot3(v, vm), m0 + 2.0 * vm, m0))
        once(2)
        once(3)
        refill(1, (1, 5))
        for side in range(2):
            halo_copy(side).wait_recv()
        fill(halo_l, GROUP, HALO)
        fill(halo_r, 6 * GROUP, HALO)
        advance(2, (1, 5))
        for g in range(4):
            imported_copy(g).wait_recv()
        for side, start in ((far_l, 0), (far_r, 6 * GROUP)):
            h, l = split(side[...])
            ie[0:FLUX, start : start + 512] = h
            ie[FLUX : 2 * FLUX, start : start + 512] = l
        for g in (0, 1, 4, 5):
            once(g)
        for g in range(4):
            h, l = split(apply(ine, g + 1, g))
            cols = slice(g * GROUP, (g + 1) * GROUP)
            fh[2 * FLUX : 3 * FLUX, cols] = h
            fl[2 * FLUX : 3 * FLUX, cols] = l
        for side in range(2):
            halo_copy(side).wait_send()
        for g in range(4):
            imported_copy(g).wait_send()

    @pl.when(c == 0)
    def _():
        coefficients((m0, jnp.zeros_like(m0), jnp.zeros_like(m0)))
        fh[FLUX : 3 * FLUX, :] = jnp.zeros((2 * FLUX, CELLS), bf16)
        fl[FLUX : 3 * FLUX, :] = jnp.zeros((2 * FLUX, CELLS), bf16)

    level = 2 * c
    for g in range(4):
        cols = slice(g * GROUP, (g + 1) * GROUP)
        a = dot(dst[...], fh[:, cols])
        out[:, cols] = states[level, :, (g + 1) * GROUP : (g + 2) * GROUP] + (
            a[0:NV] + a[NV : 2 * NV] + dot(dst[0:NV, :], fl[:, cols])
        )

    wait_send(slot_copies[2:])
    wait_send(halo0)
    wait_send(tab_copies)


def hand_over(stepped_in, imported_in, stepped, imported):
    stepped[...] = stepped_in[...]
    imported[...] = imported_in[...]


def per_device(prognostic, neighbours, diffusivity, vertical, export_map, import_map,
               ocean_mask, source_blocks, remap_index, remap_weights):
    vmem = pl.BlockSpec(memory_space=pltpu.VMEM)
    anywhere = pl.BlockSpec(memory_space=pl.ANY)
    smem = pl.BlockSpec(memory_space=pltpu.SMEM)
    dma = pltpu.SemaphoreType.DMA
    stepped, imported = pl.pallas_call(
        kernel,
        out_shape=(
            jax.ShapeDtypeStruct((NV, CELLS), f32),
            jax.ShapeDtypeStruct((FLUX, CELLS), f32),
        ),
        in_specs=[anywhere] * 7 + [smem] + [anywhere] * 2,
        out_specs=(vmem, vmem),
        scratch_shapes=[
            pltpu.VMEM((NV, CELLS), f32),
            pltpu.VMEM((NBR, 1, CELLS), jnp.int32),
            pltpu.VMEM((NBR, 1, CELLS), f32),
            pltpu.VMEM((NV, NV), f32),
            pltpu.VMEM((FLUX, NV), f32),
            pltpu.VMEM((FLUX, NV), f32),
            pltpu.VMEM((1, CELLS), jnp.int32),
            pltpu.VMEM((TAPS, CELLS), jnp.int32),
            pltpu.VMEM((TAPS, CELLS), f32),
            pltpu.VMEM((FLUX, CELLS), f32),
            pltpu.VMEM((8, FLUX, CELLS), f32),
            *[pltpu.VMEM((SOURCES * CELLS, GROUP), bf16)] * 8,
            pltpu.VMEM((TAPS, CELLS), f32),
            pltpu.VMEM((16 * TAPS, CELLS), bf16),
            pltpu.VMEM((16 * TAPS, CELLS), bf16),
            pltpu.VMEM((6, 16, GROUP), f32),
            pltpu.VMEM((6, WINDOW, GROUP), bf16),
            pltpu.VMEM((6, WINDOW, GROUP), bf16),
            pltpu.VMEM((NV, 2 * HALO), f32),
            pltpu.VMEM((NV, 2 * HALO), f32),
            pltpu.VMEM((NV, HALO), f32),
            pltpu.VMEM((NV, HALO), f32),
            pltpu.VMEM((2 * NV, 8 * GROUP), bf16),
            pltpu.VMEM((3, NV, 6 * GROUP), f32),
            pltpu.VMEM((2 * NV, NV), bf16),
            pltpu.VMEM((2 * NV, 3 * FLUX), bf16),
            pltpu.VMEM((2 * FLUX, SOURCES * CELLS), bf16),
            pltpu.VMEM((2 * FLUX, 8 * GROUP), bf16),
            pltpu.VMEM((2 * FLUX, 6 * GROUP), bf16),
            pltpu.VMEM((3 * FLUX, CELLS), bf16),
            pltpu.VMEM((3 * FLUX, CELLS), bf16),
            pltpu.VMEM((FLUX, 512), f32),
            pltpu.VMEM((FLUX, 512), f32),
            dma((9,)), dma((8, 2)), dma((8, 2)), dma((4,)), dma((4,)), dma((2,)), dma((2,)), dma((4,)), dma((4,)),
        ],
        compiler_params=pltpu.CompilerParams(
            collective_id=1, has_side_effects=True, vmem_limit_bytes=56 * 2**20
        ),
        name="coupled_interval",
    )(
        prognostic[0], jnp.transpose(neighbours, (1, 0, 2)), jnp.transpose(diffusivity, (1, 0, 2)),
        vertical[0], export_map[0], jnp.transpose(import_map[0]),
        ocean_mask, source_blocks[0], remap_index[0], remap_weights[0],
    )
    stepped, imported = pl.pallas_call(
        hand_over,
        out_shape=(
            jax.ShapeDtypeStruct((NV, CELLS), f32),
            jax.ShapeDtypeStruct((FLUX, CELLS), f32),
        ),
        name="hand_over",
    )(stepped, imported)
    return stepped[None], imported[None]


def solution(mesh):
    return jax.shard_map(
        per_device,
        mesh=mesh,
        in_specs=(
            P("comp", None, "dom"),
            P("comp", None, "dom"),
            P("comp", None, "dom"),
            P("comp", None, None),
            P("comp", None, None),
            P("comp", None, None),
            P("comp", "dom"),
            P("comp", "dom", None),
            P("comp", None, "dom"),
            P("comp", None, "dom"),
        ),
        out_specs=(P("comp", None, "dom"), P("comp", None, "dom")),
        check_vma=False,
    )
```

```python
import jax
import jax.numpy as jnp
from jax import lax
from jax.experimental import pallas as pl
from jax.experimental.pallas import tpu as pltpu
from jax.sharding import PartitionSpec as P

CELLS = 1024
NBR = 6
FLUX = 48
TAPS = 16
SOURCES = 3
NV = 144
HALO = 256
N_DOM = 64
TILE = 128
ROWS = 256
GROUP = 256
WINDOW = GROUP + 2 * HALO
PIECE = 16
PIECES = 24
UNROLL = 4
CROSSED = (12, 16, 20)
ALONG = (40, 48, 52)
AT_EDGE = (64, 68, 72)
MESH = pl.DeviceIdType.MESH
f32 = jnp.float32
bf16 = jnp.bfloat16


def split(x):
    high = x.astype(bf16)
    return high, (x - high.astype(f32)).astype(bf16)


def dot(a, b):
    return jnp.dot(a, b, preferred_element_type=f32)


def dot3(a, b):
    ah, al = split(a)
    bh, bl = split(b)
    return dot(ah, bh) + dot(al, bh) + dot(ah, bl)


def row_iota():
    return lax.broadcasted_iota(jnp.int32, (16, TILE), 0).astype(f32)


def spread(places, highs, lows, rows):
    count = rows // 16
    high = [jnp.zeros((16, TILE), bf16)] * count
    low = [jnp.zeros((16, TILE), bf16)] * count
    for place, h, l in zip(places, highs, lows):
        for r in range(count):
            hit = place == bf16(16 * r)
            high[r] = jnp.where(hit, h, high[r])
            low[r] = jnp.where(hit, l, low[r])
    return high, low


def kernel(
    prog_in, nbr_in, diff_in, vert_in, emap_in, imap_in, mask_in, blocks, ridx_in, rw_in,
    out, imported,
    prog, nbr, diff, vert, emap, imap, mask, ridx, rw,
    exported, slots, ph0, ph1, ph2, ph3, pl0, pl1, pl2, pl3, place, wh, wl,
    table, nh, nl, halo_l, halo_r, ub, states, vst, dst,
    xs, ie, ine, fh, fl, far_l, far_r,
    in_sem, slot_send, slot_recv, uh_send, uh_recv, tab_send, tab_recv, i_send, i_recv,
):
    ph = (ph0, ph1, ph2, ph3)
    pl_ = (pl0, pl1, pl2, pl3)
    c = lax.axis_index("comp")
    d = lax.axis_index("dom")
    k = lax.rem(d, 2)
    m = d // 2
    zl = lax.rem(m, 2)
    left = (c, lax.rem(d + N_DOM - 1, N_DOM))
    right = (c, lax.rem(d + 1, N_DOM))
    sibling = (c, d + 1 - 2 * k)
    along_z = (c, 2 * (m + 1 - 2 * zl) + k)
    beside = (1 - c, 2 * (m + 1 - 2 * zl) + k)
    up = lax.rem(d + 4, N_DOM)
    down = lax.rem(d + N_DOM - 4, N_DOM)

    barrier = pltpu.get_barrier_semaphore()
    for peer in (left, right, along_z, beside, (c, up), (c, down)):
        pl.semaphore_signal(barrier, inc=1, device_id=peer, device_id_type=MESH)

    inputs = [
        pltpu.make_async_copy(src, dst, in_sem.at[number])
        for number, (src, dst) in enumerate((
            (prog_in, prog), (emap_in, emap), (mask_in, mask), (nbr_in, nbr), (diff_in, diff),
            (ridx_in, ridx), (rw_in, rw), (vert_in, vert), (imap_in, imap),
        ))
    ]
    for copy in inputs:
        copy.start()
    for copy in inputs[0:3]:
        copy.wait()

    emap_h, emap_l = split(emap[...])
    est = jnp.concatenate([emap_h, emap_l], axis=0)
    for g in range(4):
        cols = pl.ds(g * GROUP, GROUP)
        uh, ul = split(prog[:, cols])
        ub[0:NV, pl.ds((g + 1) * GROUP, GROUP)] = uh
        ub[NV : 2 * NV, pl.ds((g + 1) * GROUP, GROUP)] = ul
        both = dot(est, uh)
        exported[:, cols] = mask[:, cols].astype(f32) * (
            both[0:FLUX] + both[FLUX : 2 * FLUX] + dot(emap_h, ul)
        )

    def send(src, dst, s_sem, r_sem, peer):
        copy = pltpu.make_async_remote_copy(
            src_ref=src, dst_ref=dst, send_sem=s_sem, recv_sem=r_sem,
            device_id=peer, device_id_type=MESH,
        )
        copy.start()
        return copy

    slot_copies = []

    def to_slot(src, slot, number, peer, piece):
        copy = send(
            src, slots.at[slot, pl.ds(PIECE * piece, PIECE)], slot_send.at[number, piece],
            slot_recv.at[slot, piece], peer,
        )
        slot_copies.append(copy)

    def pass_on(slot, target, number, peer, piece):
        to_slot(slots.at[slot, pl.ds(PIECE * piece, PIECE)], target, number, peer, piece)

    def arrived(slot, piece):
        rows = slots.at[slot, pl.ds(PIECE * piece, PIECE)]
        pltpu.make_async_remote_copy(
            src_ref=rows, dst_ref=rows, send_sem=slot_send.at[0, piece],
            recv_sem=slot_recv.at[slot, piece], device_id=sibling, device_id_type=MESH,
        ).wait_recv()

    own = 3 + k
    from_z = 5 + k - 4 * zl
    from_y = 1 + k + 4 * zl
    edge = 7 - 7 * k

    pl.semaphore_wait(barrier, 6)
    for piece in range(FLUX // PIECE):
        to_slot(exported.at[pl.ds(PIECE * piece, PIECE)], from_y, 0, beside, piece)

    def send_halo(source, level):
        return [
            send(source.at[:, pl.ds(0, HALO)], halo_r.at[level], uh_send.at[2 * level],
                 uh_recv.at[2 * level], left),
            send(source.at[:, pl.ds(CELLS - HALO, HALO)], halo_l.at[level], uh_send.at[2 * level + 1],
                 uh_recv.at[2 * level + 1], right),
        ]

    halo0 = send_halo(prog, 0)
    for copy in inputs[3:]:
        copy.wait()

    places = []
    weights = []
    total = jnp.zeros((1, CELLS), f32)
    for s in range(NBR):
        e = nbr[s]
        w = diff[s]
        total = total + w
        double = jnp.zeros((1, CELLS), jnp.bool_)
        for t in range(s):
            same = places[t] == e
            weights[t] = weights[t] + jnp.where(same, w, 0.0)
            double = jnp.logical_or(double, same)
        places.append(jnp.where(double, -4096, e))
        weights.append(w)
    for g in range(4):
        cols = slice(g * GROUP, (g + 1) * GROUP)
        for s in range(NBR):
            table[g + 1, s : s + 1, :] = (places[s][:, cols] - g * GROUP).astype(f32)
            table[g + 1, 8 + s : 9 + s, :] = weights[s][:, cols]
        table[g + 1, 6:7, :] = (lax.broadcasted_iota(jnp.int32, (1, GROUP), 1) + HALO).astype(f32)
        table[g + 1, 14:15, :] = 1.0 - total[:, cols]
    tab_copies = [
        send(table.at[4], table.at[0], tab_send.at[0], tab_recv.at[0], right),
        send(table.at[1], table.at[5], tab_send.at[1], tab_recv.at[1], left),
    ]

    idx = ridx[...]
    w = rw[...]
    tap = lax.broadcasted_iota(jnp.int32, (TAPS, CELLS), 0)
    total_w = w
    double = tap < 0
    for s in range(1, TAPS):
        same = idx == pltpu.roll(idx, s, 0)
        total_w = total_w + jnp.where(same, pltpu.roll(w, s, 0), 0.0)
        double = jnp.logical_or(double, jnp.logical_and(same, tap >= s))
    place[...] = jnp.where(double, -4096, idx).astype(f32)
    for t in range(TAPS):
        h, l = split(jnp.broadcast_to(total_w[t : t + 1, :], (16, CELLS)))
        wh[16 * t : 16 * t + 16, :] = h
        wl[16 * t : 16 * t + 16, :] = l

    def relative(row, base):
        return (jnp.broadcast_to(row, (16, TILE)) - base).astype(bf16) - row_iota().astype(bf16)

    def remap_chunk(i, group):
        i = i - PIECES * group
        half = i // (PIECES // 2)
        row = lax.rem(i, PIECES // 2) * ROWS
        cols = pl.ds(pl.multiple_of(half * TILE, TILE), TILE)
        wide = pl.ds(pl.multiple_of(group * GROUP + half * TILE, TILE), TILE)
        base = row.astype(f32)
        high, low = spread(
            [relative(place[t : t + 1, wide], base) for t in range(TAPS)],
            [wh[16 * t : 16 * t + 16, wide] for t in range(TAPS)],
            [wl[16 * t : 16 * t + 16, wide] for t in range(TAPS)],
            ROWS,
        )
        for r in range(ROWS // 16):
            rows = pl.ds(pl.multiple_of(row + 16 * r, 16), 16)
            ph[group][rows, cols] = high[r]
            pl_[group][rows, cols] = low[r]

    def build_remap(first, last):
        for group in range(4):
            def chunk(i, carry):
                for j in range(UNROLL):
                    remap_chunk(UNROLL * i + j, group)
                return carry

            low = max(first, PIECES * group)
            high = min(last, PIECES * (group + 1))
            if low < high:
                lax.fori_loop(low // UNROLL, high // UNROLL, chunk, 0)

    def build_neighbour(g):
        def part(half, carry):
            cols = pl.ds(pl.multiple_of(half * TILE, TILE), TILE)
            start = half * TILE
            base = start.astype(f32)
            split_weights = [
                split(jnp.broadcast_to(table[g, 8 + s : 9 + s, cols], (16, TILE)))
                for s in range(NBR + 1)
            ]
            for block in range(5):
                taps = NBR + 1 if block == 2 else NBR
                high, low = spread(
                    [relative(table[g, s : s + 1, cols], base + 128.0 * block) for s in range(taps)],
                    [split_weights[s][0] for s in range(taps)],
                    [split_weights[s][1] for s in range(taps)],
                    TILE,
                )
                for r in range(TILE // 16):
                    rows = pl.ds(pl.multiple_of(start + TILE * block + 16 * r, 16), 16)
                    nh[g, rows, cols] = high[r]
                    nl[g, rows, cols] = low[r]
            rest = pl.ds(pl.multiple_of((1 - half) * 5 * TILE, TILE), TILE)
            nh[g, rest, cols] = jnp.zeros((TILE, TILE), bf16)
            nl[g, rest, cols] = jnp.zeros((TILE, TILE), bf16)
            return carry

        lax.fori_loop(0, 2, part, 0)

    vh, vl = split(vert[...])
    vst[0:NV, :] = vh
    vst[NV : 2 * NV, :] = vl

    def advance(level, first=0, beside_it=0):
        for side, start in ((halo_l, 0), (halo_r, 5 * GROUP)):
            h, l = split(side[level])
            ub[0:NV, pl.ds(start, GROUP)] = h
            ub[NV : 2 * NV, pl.ds(start, GROUP)] = l

        def group(g, carry):
            window = pl.ds(pl.multiple_of(g * GROUP, GROUP), WINDOW)
            mid = pl.ds(pl.multiple_of((g + 1) * GROUP, GROUP), GROUP)
            a = dot(ub[:, window], nh[g + 1])
            b = dot(vst[...], ub[0:NV, mid])
            total = a[0:NV] + a[NV : 2 * NV] + dot(ub[0:NV, window], nl[g + 1])
            total = total + (b[0:NV] + b[NV : 2 * NV] + dot(vst[0:NV, :], ub[NV : 2 * NV, mid]))
            states[level, :, pl.ds(pl.multiple_of(g * GROUP, GROUP), GROUP)] = total
            for j in range(beside_it):
                remap_chunk(first + beside_it * g + j, first // PIECES)
            return carry

        lax.fori_loop(0, 4, group, 0, unroll=beside_it == 0)

    def refill(level):
        def group(g, carry):
            mid = pl.ds(pl.multiple_of((g + 1) * GROUP, GROUP), GROUP)
            h, l = split(states[level, :, pl.ds(pl.multiple_of(g * GROUP, GROUP), GROUP)])
            ub[0:NV, mid] = h
            ub[NV : 2 * NV, mid] = l
            return carry

        lax.fori_loop(0, 4, group, 0, unroll=True)

    def wait_recv(copies):
        for copy in copies:
            copy.wait_recv()

    def wait_send(copies):
        for copy in copies:
            copy.wait_send()

    for g in range(1, 5):
        build_neighbour(g)

    def crossed(piece):
        arrived(from_z, piece)
        pass_on(from_z, own, 1, along_z, piece)
        pass_on(from_z, from_y, 2, (c, lax.select(zl == 0, up, down)), piece)
        pass_on(from_z, from_z, 3, sibling, piece)

    def spread_along_y(piece):
        arrived(own, piece)
        pass_on(own, edge, 4, (c, lax.select(k == 1, up, down)), piece)
        pass_on(own, own, 5, sibling, piece)
        arrived(from_y, piece)
        pass_on(from_y, from_y, 6, sibling, piece)

    def shared(piece):
        arrived(edge, piece)
        pass_on(edge, edge, 7, sibling, piece)

    done = 0
    for piece, place_in_plan in enumerate(CROSSED):
        build_remap(done, place_in_plan)
        done = place_in_plan
        crossed(piece)
    wait_recv(halo0)
    build_remap(done, 24)
    advance(0, 24, 4)

    @pl.when(c == 1)
    def _():
        send_halo(states.at[0], 1)

    done = 40
    for step, plan in ((spread_along_y, ALONG), (shared, AT_EDGE)):
        for piece, place_in_plan in enumerate(plan):
            build_remap(done, place_in_plan)
            done = place_in_plan
            step(piece)

    def halo_copy(level, side):
        return pltpu.make_async_remote_copy(
            src_ref=states.at[level - 1, :, pl.ds((CELLS - HALO) * side, HALO)],
            dst_ref=(halo_r, halo_l)[side].at[level],
            send_sem=uh_send.at[2 * level + side], recv_sem=uh_recv.at[2 * level + side],
            device_id=(left, right)[side], device_id_type=MESH,
        )

    def halo_arrived(level):
        for side in range(2):
            halo_copy(level, side).wait_recv()

    @pl.when(c == 0)
    def _():
        build_remap(72, 84)

    @pl.when(c == 1)
    def _():
        refill(0)
        halo_arrived(1)
        advance(1, 72, 3)
        send_halo(states.at[1], 2)

    m0 = imap[...].T

    def coefficients(values):
        for number, value in enumerate(values):
            h, l = split(value)
            cols = slice(FLUX * number, FLUX * (number + 1))
            dst[0:NV, cols] = h
            dst[NV : 2 * NV, cols] = l

    other = 1 - k
    for piece in range(FLUX // PIECE):
        arrived(3 + other, piece)
        arrived(5 + other - 4 * zl, piece)
        arrived(1 + other + 4 * zl, piece)
        arrived(7 - 7 * other, piece)

    for r in range(SOURCES):
        slot = jnp.minimum(lax.rem(blocks[0, r] - 2 * m + 3 + N_DOM, N_DOM), 7)
        h, l = split(slots[slot])
        xs[0:FLUX, r * CELLS : (r + 1) * CELLS] = h
        xs[FLUX : 2 * FLUX, r * CELLS : (r + 1) * CELLS] = l

    wait_send(slot_copies[0 : FLUX // PIECE])

    def remap_beside(g):
        cols = slice(g * GROUP, (g + 1) * GROUP)
        exported[:, cols] = jnp.zeros((FLUX, GROUP), f32)

        def step(j, carry):
            depth = pl.ds(pl.multiple_of(j * 768, 768), 768)
            a = dot(xs[:, depth], ph[g][depth, :])
            exported[:, cols] += a[0:FLUX] + a[FLUX : 2 * FLUX] + dot(xs[0:FLUX, depth], pl_[g][depth, :])
            remap_chunk(84 + 4 * g + j, 3)
            return carry

        lax.fori_loop(0, 4, step, 0)

    def remap_last():
        a = dot(xs[...], ph[3][...])
        exported[:, 3 * GROUP :] = a[0:FLUX] + a[FLUX : 2 * FLUX] + dot(xs[0:FLUX, :], pl_[3][...])

    def keep(g):
        cols = slice(g * GROUP, (g + 1) * GROUP)
        value = exported[:, cols]
        imported[:, cols] = value
        h, l = split(value)
        mid = slice((g + 2) * GROUP, (g + 3) * GROUP)
        ie[0:FLUX, mid] = h
        ie[FLUX : 2 * FLUX, mid] = l
        fh[0:FLUX, cols] = h
        fl[0:FLUX, cols] = l

    def imported_copy(g):
        side = g // 2
        cols = pl.ds(GROUP * g, GROUP)
        there = pl.ds(GROUP * (g - 2 * side), GROUP)
        return pltpu.make_async_remote_copy(
            src_ref=exported.at[:, cols], dst_ref=(far_r, far_l)[side].at[:, there],
            send_sem=i_send.at[g], recv_sem=i_recv.at[g],
            device_id=(left, right)[side], device_id_type=MESH,
        )

    def start_imported(g):
        @pl.when(c == 1)
        def _():
            imported_copy(g).start()

    for g in range(3):
        remap_beside(g)
        start_imported(g)
    remap_last()
    start_imported(3)
    for g in range(4):
        keep(g)

    def apply(source, matrix, g):
        window = slice(g * GROUP, g * GROUP + WINDOW)
        a = dot(source[:, window], nh[matrix])
        return a[0:FLUX] + a[FLUX : 2 * FLUX] + dot(source[0:FLUX, window], nl[matrix])

    def once(g):
        h, l = split(apply(ie, g, g))
        cols = slice(g * GROUP, (g + 1) * GROUP)
        ine[0:FLUX, cols] = h
        ine[FLUX : 2 * FLUX, cols] = l
        if 1 <= g < 5:
            mid = slice((g - 1) * GROUP, g * GROUP)
            fh[FLUX : 2 * FLUX, mid] = h
            fl[FLUX : 2 * FLUX, mid] = l

    @pl.when(c == 1)
    def _():
        refill(1)
        halo_arrived(2)
        advance(2)
        v = vert[...]
        vm = dot3(v, m0)
        coefficients((m0 + vm + dot3(v, vm), m0 + 2.0 * vm, m0))
        wait_recv(tab_copies)
        build_neighbour(0)
        build_neighbour(5)
        once(2)
        once(3)
        for g in range(4):
            imported_copy(g).wait_recv()
        for side, start in ((far_l, 0), (far_r, 6 * GROUP)):
            h, l = split(side[...])
            ie[0:FLUX, start : start + 512] = h
            ie[FLUX : 2 * FLUX, start : start + 512] = l
        for g in (0, 1, 4, 5):
            once(g)
        for g in range(4):
            h, l = split(apply(ine, g + 1, g))
            cols = slice(g * GROUP, (g + 1) * GROUP)
            fh[2 * FLUX : 3 * FLUX, cols] = h
            fl[2 * FLUX : 3 * FLUX, cols] = l
        for side in range(2):
            halo_copy(1, side).wait_send()
            halo_copy(2, side).wait_send()
        for g in range(4):
            imported_copy(g).wait_send()

    @pl.when(c == 0)
    def _():
        coefficients((m0, jnp.zeros_like(m0), jnp.zeros_like(m0)))
        fh[FLUX : 3 * FLUX, :] = jnp.zeros((2 * FLUX, CELLS), bf16)
        fl[FLUX : 3 * FLUX, :] = jnp.zeros((2 * FLUX, CELLS), bf16)
        wait_recv(tab_copies)

    level = 2 * c
    for g in range(4):
        cols = slice(g * GROUP, (g + 1) * GROUP)
        a = dot(dst[...], fh[:, cols])
        out[:, cols] = states[level, :, cols] + (
            a[0:NV] + a[NV : 2 * NV] + dot(dst[0:NV, :], fl[:, cols])
        )

    wait_send(slot_copies[FLUX // PIECE :])
    wait_send(halo0)
    wait_send(tab_copies)


def hand_over(stepped_in, imported_in, stepped, imported):
    stepped[...] = stepped_in[...]
    imported[...] = imported_in[...]


def per_device(prognostic, neighbours, diffusivity, vertical, export_map, import_map,
               ocean_mask, source_blocks, remap_index, remap_weights):
    vmem = pl.BlockSpec(memory_space=pltpu.VMEM)
    anywhere = pl.BlockSpec(memory_space=pl.ANY)
    smem = pl.BlockSpec(memory_space=pltpu.SMEM)
    dma = pltpu.SemaphoreType.DMA
    stepped, imported = pl.pallas_call(
        kernel,
        out_shape=(
            jax.ShapeDtypeStruct((NV, CELLS), f32),
            jax.ShapeDtypeStruct((FLUX, CELLS), f32),
        ),
        in_specs=[anywhere] * 7 + [smem] + [anywhere] * 2,
        out_specs=(vmem, vmem),
        scratch_shapes=[
            pltpu.VMEM((NV, CELLS), f32),
            pltpu.VMEM((NBR, 1, CELLS), jnp.int32),
            pltpu.VMEM((NBR, 1, CELLS), f32),
            pltpu.VMEM((NV, NV), f32),
            pltpu.VMEM((FLUX, NV), f32),
            pltpu.VMEM((FLUX, NV), f32),
            pltpu.VMEM((1, CELLS), jnp.int32),
            pltpu.VMEM((TAPS, CELLS), jnp.int32),
            pltpu.VMEM((TAPS, CELLS), f32),
            pltpu.VMEM((FLUX, CELLS), f32),
            pltpu.VMEM((8, FLUX, CELLS), f32),
            *[pltpu.VMEM((SOURCES * CELLS, GROUP), bf16)] * 8,
            pltpu.VMEM((TAPS, CELLS), f32),
            pltpu.VMEM((16 * TAPS, CELLS), bf16),
            pltpu.VMEM((16 * TAPS, CELLS), bf16),
            pltpu.VMEM((6, 16, GROUP), f32),
            pltpu.VMEM((6, WINDOW, GROUP), bf16),
            pltpu.VMEM((6, WINDOW, GROUP), bf16),
            pltpu.VMEM((3, NV, HALO), f32),
            pltpu.VMEM((3, NV, HALO), f32),
            pltpu.VMEM((2 * NV, 6 * GROUP), bf16),
            pltpu.VMEM((3, NV, CELLS), f32),
            pltpu.VMEM((2 * NV, NV), bf16),
            pltpu.VMEM((2 * NV, 3 * FLUX), bf16),
            pltpu.VMEM((2 * FLUX, SOURCES * CELLS), bf16),
            pltpu.VMEM((2 * FLUX, 8 * GROUP), bf16),
            pltpu.VMEM((2 * FLUX, 6 * GROUP), bf16),
            pltpu.VMEM((3 * FLUX, CELLS), bf16),
            pltpu.VMEM((3 * FLUX, CELLS), bf16),
            pltpu.VMEM((FLUX, 512), f32),
            pltpu.VMEM((FLUX, 512), f32),
            dma((9,)), dma((8, FLUX // PIECE)), dma((8, FLUX // PIECE)), dma((6,)), dma((6,)), dma((2,)), dma((2,)), dma((4,)), dma((4,)),
        ],
        compiler_params=pltpu.CompilerParams(
            collective_id=1, has_side_effects=True, vmem_limit_bytes=56 * 2**20
        ),
        name="coupled_interval",
    )(
        prognostic[0], jnp.transpose(neighbours, (1, 0, 2)), jnp.transpose(diffusivity, (1, 0, 2)),
        vertical[0], export_map[0], jnp.transpose(import_map[0]),
        ocean_mask, source_blocks[0], remap_index[0], remap_weights[0],
    )
    stepped, imported = pl.pallas_call(
        hand_over,
        out_shape=(
            jax.ShapeDtypeStruct((NV, CELLS), f32),
            jax.ShapeDtypeStruct((FLUX, CELLS), f32),
        ),
        name="hand_over",
    )(stepped, imported)
    return stepped[None], imported[None]


def solution(mesh):
    return jax.shard_map(
        per_device,
        mesh=mesh,
        in_specs=(
            P("comp", None, "dom"),
            P("comp", None, "dom"),
            P("comp", None, "dom"),
            P("comp", None, None),
            P("comp", None, None),
            P("comp", None, None),
            P("comp", "dom"),
            P("comp", "dom", None),
            P("comp", None, "dom"),
            P("comp", None, "dom"),
        ),
        out_specs=(P("comp", None, "dom"), P("comp", None, "dom")),
        check_vma=False,
    )
```
